32 devices in a mesh: grp: 4 (over y, x), dom: 8 (over z, core).
Axes of the slice: x: 2, y: 2, z: 4, core: 2. Of those that a mesh axis runs over, the one named last changes fastest.
Arguments:
- features: bfloat16 [8192, 256], P(('grp', 'dom')), may hold values from -6 to 6
- cotangent: bfloat16 [8192, 256], P(('grp', 'dom')), may hold values from -6 to 6
- weight_self: bfloat16 [256, 256], replicated, may hold values from -0.375 to 0.375
- weight_neigh: bfloat16 [256, 256], replicated, may hold values from -0.375 to 0.375
- layer_bias: bfloat16 [256], replicated, may hold values from -3 to 3
- mirror_rows: int32 [32, 32, 32], P(('grp', 'dom')), may hold values from 0 to 255
- mirror_counts: int32 [32, 32], replicated, may hold values from 1 to 32, 768 in all within a row
- tile_count: int32 [32], P(('grp', 'dom')), may hold values from 1 to 320, 4480 in all
- tile_rows: int32 [32, 320], P(('grp', 'dom')), may hold values from 0 to 7
- tile_cols: int32 [32, 320], P(('grp', 'dom')), may hold values from 0 to 7
- tile_masks: int32 [32, 320, 128, 128], P(('grp', 'dom')), may hold values 0 or 1
Outputs:
- output: bfloat16 [8192, 256], P(('grp', 'dom'))
- grad_x: bfloat16 [8192, 256], P(('grp', 'dom'))
- grad_self: float32 [256, 256], replicated
- grad_neigh: float32 [256, 256], replicated
- grad_bias: float32 [256], replicated
The draws below stay inside these ranges and needn't reach their ends.
Inputs may be any that keep to these rules, and one draw needn't show every extreme that they name: `mirror_rows`: only entries with c < mirror_counts[d, s] name live mirrors; the others are unused. `mirror_counts`: each row sums to 768 and holds 32 in some entry. `tile_count`: some device uses all 320 tile slots; the counts sum to 4480.
All inputs are finite; a program needn't handle non-finite values. No bound on the sum of `tile_masks` on one device may be relied on, other than what follows from the above.
Results may differ from the reference program's by a relative error of at most 0.0075.
Values may be sent and summed in bfloat16 or wider, within the bound.
No kernel may reach another device: no remote copies, remote signals or barrier semaphores. Data moves between devices by JAX's collectives and lax.ppermute only.
A program may use at most 128 MiB of HBM per device.

```python
import math
import jax
import jax.numpy as jnp
import numpy as np
from jax import lax

D_IN = 256
D_OUT = 256
TILE = 128
V_DEV = 256
TILES_MAX = 320
SHARDS = 32
VERTICES = 8192
CAP = 32
SLOTS = 1024
BLOCKS = 8
TILES_MEAN = 140


def with_ends(drawn, key, smallest, high):
    longest = drawn.shape.index(max(drawn.shape))
    spots = []
    for shift in (0, 1):
        where = [jax.random.randint(jax.random.fold_in(key, axis), (), 0, length) for axis, length in enumerate(drawn.shape)]
        where[longest] = (where[longest] + shift) % drawn.shape[longest]
        spots.append(tuple(where))
    return drawn.at[spots[0]].set(smallest).at[spots[1]].set(high)


def level_of(key, dims, pieces, least, top_value):
    factor_of, own = 1.0, jax.random.fold_in(key, 6)
    for axis_at, parts in pieces:
        draws = jnp.exp(jax.random.uniform(jax.random.fold_in(own, axis_at), (parts,), jnp.float32, least / len(pieces), top_value / len(pieces)))
        factor_of = factor_of * jnp.repeat(draws, dims[axis_at] // parts).reshape([-1 if axis == axis_at else 1 for axis in range(len(dims))])
    return factor_of


def profile(count, total, reach, lean):
    portions = [(1 << 20) // math.isqrt(grade ** lean) + 1 for grade in range(2, count + 1)]
    surplus, counts = total - reach - (count - 1), [1] * (count - 1)
    while surplus > 0:
        free = [i for i in range(count - 1) if counts[i] < reach]
        mass, remaining = sum([portions[i] for i in free]), surplus
        for i in free:
            more = min(reach - counts[i], max(1, remaining * portions[i] // mass), surplus)
            counts[i] = counts[i] + more
            surplus = surplus - more
    return np.array([reach] + counts)


def ragged(key, number_of, total, limit, lean):
    if number_of == 2:
        one = jax.random.randint(key, (), max(1, total - limit), min(limit, total - 1) + 1)
        return jnp.stack([one, total - one])
    lengths = jnp.asarray(profile(number_of, total, limit, lean), jnp.int32)
    couples = (number_of - 1) // 2
    source_of, receiver = lengths[1:1 + 2 * couples:2], lengths[2:2 + 2 * couples:2]
    slack = jnp.minimum(source_of - 1, limit - receiver)
    moved = jax.random.randint(jax.random.fold_in(key, 1), (couples,), 0, 1 << 20) % (slack + 1)
    lengths = lengths.at[1:1 + 2 * couples:2].set(source_of - moved).at[2:2 + 2 * couples:2].set(receiver + moved)
    return lengths[jax.random.permutation(jax.random.fold_in(key, 2), number_of)]


def normal_values(rng, extent, scale, most, pieces=(), kind=jnp.bfloat16):
    gain = level_of(rng, extent, pieces, -0.22, 0.18) if pieces else 1.0
    values = jax.random.normal(rng, extent, jnp.float32) * scale * gain
    return jnp.minimum(jnp.maximum(values, -most), most).astype(kind)


def setup_inputs(seed: int = 0) -> dict:
    key_list = jax.random.split(jax.random.key(seed), 12)
    return {
        "features": normal_values(key_list[0], (VERTICES, D_IN), 1.0, 6.0, ((0, 32),)),
        "cotangent": normal_values(key_list[1], (VERTICES, D_OUT), 1.0, 6.0, ((0, 32),)),
        "weight_self": normal_values(key_list[2], (D_IN, D_OUT), D_IN ** -0.5, 0.375),
        "weight_neigh": normal_values(key_list[3], (D_IN, D_OUT), D_IN ** -0.5, 0.375),
        "layer_bias": normal_values(key_list[4], (D_OUT,), 0.5, 3.0),
        "mirror_rows": with_ends(jax.random.randint(key_list[5], (SHARDS, SHARDS, CAP), 0, V_DEV), jax.random.fold_in(key_list[5], 1), 0, V_DEV - 1).astype(jnp.int32),
        "mirror_counts": jax.vmap(lambda own: ragged(own, SHARDS, 3 * V_DEV, CAP, 1))(jax.random.split(key_list[6], SHARDS)).reshape((SHARDS, SHARDS)).astype(jnp.int32),
        "tile_count": ragged(key_list[7], SHARDS, TILES_MEAN * SHARDS, TILES_MAX, 2).astype(jnp.int32),
        "tile_rows": with_ends(jax.random.randint(key_list[8], (SHARDS, TILES_MAX), 0, BLOCKS), jax.random.fold_in(key_list[8], 1), 0, BLOCKS - 1).astype(jnp.int32),
        "tile_cols": with_ends(jax.random.randint(key_list[9], (SHARDS, TILES_MAX), 0, BLOCKS), jax.random.fold_in(key_list[9], 1), 0, BLOCKS - 1).astype(jnp.int32),
        "tile_masks": with_ends((jax.random.randint(key_list[10], (SHARDS, TILES_MAX, TILE, TILE), 0, TILES_MEAN * TILE) < min(6 * BLOCKS, TILES_MEAN * TILE // 2)).astype(jnp.int32), jax.random.fold_in(key_list[10], 1), 0, 1),
    }


def tile_sweep(masks_here, dst_blocks, src_blocks, used_tiles, source, transpose):
    per_turn = min(16, TILES_MAX)
    initial = jnp.zeros(source.shape, jnp.float32)

    def one_turn(turn_index, totals):
        first_tile = (turn_index * per_turn).astype(jnp.int32)
        masks_turn = lax.dynamic_slice_in_dim(masks_here, first_tile, per_turn, 0).astype(jnp.float32)
        dst_turn = lax.dynamic_slice_in_dim(dst_blocks, first_tile, per_turn, 0)
        src_turn = lax.dynamic_slice_in_dim(src_blocks, first_tile, per_turn, 0)
        in_use = (first_tile + jnp.arange(per_turn, dtype=jnp.int32) < used_tiles).astype(jnp.float32)
        if transpose:
            terms = jnp.einsum('tij,tif->tjf', masks_turn, source[dst_turn])
            return totals.at[src_turn].add(terms * in_use[:, None, None])
        terms = jnp.einsum('tij,tjf->tif', masks_turn, source[src_turn])
        return totals.at[dst_turn].add(terms * in_use[:, None, None])
    turns = ((used_tiles + per_turn - 1) // per_turn).astype(jnp.int32)
    return lax.fori_loop(jnp.int32(0), turns, one_turn, initial)

def slot_live(count_row):
    flags = jnp.arange(CAP, dtype=jnp.int32)[None, :] < count_row[:, None]
    return flags.reshape(SLOTS).astype(jnp.float32)

def reference(features, cotangent, weight_self, weight_neigh, layer_bias, mirror_rows, mirror_counts, tile_count, tile_rows, tile_cols, tile_masks):
    by_owner = features.reshape(SHARDS, V_DEV, D_IN)
    owners = jnp.arange(SHARDS, dtype=jnp.int32)[:, None]
    receive_rows = jnp.swapaxes(mirror_rows, 0, 1)
    items = (receive_rows, mirror_counts, tile_count, tile_rows, tile_cols, tile_masks)

    def forward_device(carry, entry):
        master_sums, degrees = carry
        rows_here, count_row, used_tiles, dst_blocks, src_blocks, masks_here = entry
        live_slot = slot_live(count_row)
        mirrored = by_owner[owners, rows_here].reshape(SLOTS, D_IN).astype(jnp.float32) * live_slot[:, None]
        partial_value = tile_sweep(masks_here, dst_blocks, src_blocks, used_tiles, mirrored.reshape(BLOCKS, TILE, D_IN), False)
        partial_value = partial_value.reshape(SLOTS, D_IN) * live_slot[:, None]
        counted = tile_sweep(masks_here, dst_blocks, src_blocks, used_tiles, live_slot.reshape(BLOCKS, TILE, 1), False)
        counted = counted.reshape(SLOTS) * live_slot
        master_sums = master_sums.at[owners, rows_here].add(partial_value.reshape(SHARDS, CAP, D_IN))
        degrees = degrees.at[owners, rows_here].add(counted.reshape(SHARDS, CAP))
        return ((master_sums, degrees), None)
    start_sums = (jnp.zeros((SHARDS, V_DEV, D_IN), jnp.float32), jnp.zeros((SHARDS, V_DEV), jnp.float32))
    forward_out = lax.scan(forward_device, start_sums, items)
    master_sums, degrees = forward_out[0]
    divisor = jnp.maximum(degrees.reshape(VERTICES), 1.0)
    mean_rows = (master_sums.reshape(VERTICES, D_IN) / divisor[:, None]).astype(jnp.bfloat16)
    pre_act = jnp.dot(features, weight_self, preferred_element_type=jnp.float32) + jnp.dot(mean_rows, weight_neigh, preferred_element_type=jnp.float32) + layer_bias.astype(jnp.float32)
    output = jax.nn.silu(pre_act).astype(jnp.bfloat16)
    sigmoid_pre = jax.nn.sigmoid(pre_act)
    grad_pre = (cotangent.astype(jnp.float32) * sigmoid_pre * (1.0 + pre_act * (1.0 - sigmoid_pre))).astype(jnp.bfloat16)
    norm_scale = 1.0 / math.sqrt(VERTICES)
    grad_self = jnp.dot(features.T, grad_pre, preferred_element_type=jnp.float32) * norm_scale
    grad_neigh = jnp.dot(mean_rows.T, grad_pre, preferred_element_type=jnp.float32) * norm_scale
    grad_bias = lax.optimization_barrier(jnp.sum(grad_pre.astype(jnp.float32), axis=0)) * norm_scale
    grad_mean = (jnp.dot(grad_pre, weight_neigh.T, preferred_element_type=jnp.float32) / divisor[:, None]).astype(jnp.bfloat16)
    grad_self_x = jnp.dot(grad_pre, weight_self.T, preferred_element_type=jnp.float32)
    grads_owner = grad_mean.reshape(SHARDS, V_DEV, D_IN)

    def backward_device(back_sums, entry):
        rows_here, count_row, used_tiles, dst_blocks, src_blocks, masks_here = entry
        live_slot = slot_live(count_row)
        mirrored_grads = grads_owner[owners, rows_here].reshape(SLOTS, D_IN).astype(jnp.float32) * live_slot[:, None]
        back_partial = tile_sweep(masks_here, dst_blocks, src_blocks, used_tiles, mirrored_grads.reshape(BLOCKS, TILE, D_IN), True)
        back_partial = back_partial.reshape(SLOTS, D_IN) * live_slot[:, None]
        back_sums = back_sums.at[owners, rows_here].add(back_partial.reshape(SHARDS, CAP, D_IN))
        return (back_sums, None)
    backward_out = lax.scan(backward_device, jnp.zeros((SHARDS, V_DEV, D_IN), jnp.float32), items)
    back_sum = backward_out[0].reshape(VERTICES, D_IN)
    grad_x = (grad_self_x + back_sum).astype(jnp.bfloat16)
    return (output, grad_x, grad_self, grad_neigh, grad_bias)
```

```python
import functools
import math

import jax
import jax.numpy as jnp
from jax import lax
from jax.experimental import pallas as pl
from jax.experimental.pallas import tpu as pltpu
from jax.sharding import PartitionSpec as P

AXES = ("grp", "dom")
LANES = 128
EXACT = 256
MIB = 1 << 20

NT = (((1,), (1,)), ((), ()))
TN = (((0,), (0,)), ((), ()))


def dot32(a, b):
    return jnp.dot(a, b, preferred_element_type=jnp.float32)


def dot_general32(a, b, dims):
    return lax.dot_general(a, b, dims, preferred_element_type=jnp.float32)


def iota(shape, dim):
    return lax.broadcasted_iota(jnp.int32, shape, dim)


def rows_2d(block):
    peers, rows, width = block.shape
    if rows % 16 == 0:
        return block.reshape(peers * rows, width)
    return block.astype(jnp.float32).reshape(peers * rows, width).astype(block.dtype)


def rows_3d(block, rows):
    return block.reshape(block.shape[0] // rows, rows, block.shape[1]).astype(jnp.bfloat16)


def diagonal_row(spread, capacity):
    peers, slots = spread.shape
    own = iota((peers, slots), 1) // capacity == iota((peers, slots), 0)
    return jnp.sum(jnp.where(own, spread, 0.0), axis=0, keepdims=True)


def one_hot(index_row, v_local):
    slots = index_row.shape[1]
    return (iota((v_local, slots), 0) == index_row).astype(jnp.float32).astype(jnp.bfloat16)


def gather_kernel(me_ref, rows_ref, counts_ref, features_ref, index_ref, outgoing_ref):
    peers, capacity = rows_ref.shape[1:]
    slots = peers * capacity
    v_local = features_ref.shape[0]
    mine = iota((peers, peers), 1) == me_ref[0]
    live_count = jnp.sum(jnp.where(mine, counts_ref[...], 0), axis=1, keepdims=True)
    live = iota((peers, capacity), 1) < live_count
    index = jnp.where(live, rows_ref[0], -1).astype(jnp.float32).astype(jnp.bfloat16)
    place = iota((capacity, slots), 1) % capacity == iota((capacity, slots), 0)
    spread = dot32(index, place.astype(jnp.float32).astype(jnp.bfloat16))
    index_row = diagonal_row(spread, capacity).astype(jnp.int32)
    index_ref[...] = index_row
    picked = dot_general32(one_hot(index_row, v_local), features_ref[...], TN)
    outgoing_ref[...] = rows_3d(picked, capacity)


def build_kernel(
    buffers,
    chunk,
    me_ref,
    used_ref,
    dst_ref,
    src_ref,
    counts_ref,
    masks_ref,
    adj_ref,
    adj_t_ref,
    counted_ref,
    over_ref,
    rest_ref,
    total,
    held,
    stage,
    sems,
    stage_sem,
):
    peers = counts_ref.shape[0]
    tile = masks_ref.shape[1]
    slots = adj_ref.shape[0]
    blocks = slots // tile
    capacity = slots // peers
    used = used_ref[0]
    chunks = (used + chunk - 1) // chunk

    def fetch(step):
        slot = lax.rem(step, buffers)
        return pltpu.make_async_copy(
            masks_ref.at[pl.ds(step * chunk, chunk)], held.at[slot], sems.at[slot]
        )

    for step in range(buffers):

        @pl.when(step < chunks)
        def _():
            fetch(step).start()

    def clear(block, carry):
        total[block] = jnp.zeros((tile, tile), jnp.int32)
        return carry

    lax.fori_loop(0, blocks * blocks, clear, 0)

    def one_chunk(step, carry):
        slot = lax.rem(step, buffers)
        fetch(step).wait()
        first = step * chunk

        def one_tile(at, inner):
            where = dst_ref[0, first + at] * blocks + src_ref[0, first + at]
            total[where] += held[slot, at]
            return inner

        full = first + chunk <= used

        @pl.when(full)
        def _():
            for at in range(chunk):
                one_tile(at, 0)

        @pl.when(jnp.logical_not(full))
        def _():
            lax.fori_loop(0, used - first, one_tile, 0)

        @pl.when(step + buffers < chunks)
        def _():
            fetch(step + buffers).start()

        return carry

    lax.fori_loop(0, chunks, one_chunk, 0)

    mine = iota((peers, peers), 0) == me_ref[0]
    live_count = jnp.sum(jnp.where(mine, counts_ref[...], 0), axis=0, keepdims=True)
    live_count = jnp.broadcast_to(live_count, (8, peers)).astype(jnp.float32)
    place = iota((peers, slots), 1) // capacity == iota((peers, slots), 0)
    spread = dot32(
        live_count.astype(jnp.bfloat16), place.astype(jnp.float32).astype(jnp.bfloat16)
    )
    live_row = (iota((8, slots), 1) % capacity < spread.astype(jnp.int32)).astype(jnp.float32)

    def one_row(row, most):
        counted = jnp.zeros((tile, tile), jnp.float32)
        at_row = pl.multiple_of(row * tile, tile)
        for col in range(blocks):
            value = total[row * blocks + col]
            most = jnp.maximum(most, value)
            value = value.astype(jnp.float32)
            counted = counted + value * live_row[:1, col * tile : (col + 1) * tile]
            low = jnp.minimum(value, float(EXACT))
            adj_ref[pl.ds(at_row, tile), col * tile : (col + 1) * tile] = low.astype(jnp.bfloat16)
            adj_t_ref[col * tile : (col + 1) * tile, pl.ds(at_row, tile)] = low.T.astype(
                jnp.bfloat16
            )
        counted_ref[pl.ds(row, 1), :] = jnp.sum(counted.T, axis=0, keepdims=True)
        return most

    most = lax.fori_loop(0, blocks, one_row, jnp.zeros((tile, tile), jnp.int32))
    over = jnp.max(most) > EXACT
    over_ref[0] = over.astype(jnp.int32)

    @pl.when(over)
    def _():
        def rest_row(row, carry):
            for col in range(blocks):
                value = jnp.maximum(total[row * blocks + col] - EXACT, 0)
                stage[:, col * tile : (col + 1) * tile] = value.astype(jnp.float32).astype(
                    jnp.bfloat16
                )
            copy = pltpu.make_async_copy(
                stage, rest_ref.at[pl.ds(pl.multiple_of(row * tile, tile), tile)], stage_sem
            )
            copy.start()
            copy.wait()
            return carry

        lax.fori_loop(0, blocks, rest_row, 0)


def forward_kernel(
    over_ref, adj_ref, counted_ref, mirrored_ref, rest_ref, out_ref, sums, stage, stage_sem
):
    peers, capacity, width = mirrored_ref.shape
    slots = peers * capacity
    tile = stage.shape[0]
    source = rows_2d(mirrored_ref[...])
    sums[...] = dot32(adj_ref[...], source)

    @pl.when(over_ref[0] != 0)
    def _():
        def rest_row(row, carry):
            at_row = pl.multiple_of(row * tile, tile)
            copy = pltpu.make_async_copy(rest_ref.at[pl.ds(at_row, tile)], stage, stage_sem)
            copy.start()
            copy.wait()
            sums[pl.ds(at_row, tile), :] += dot32(stage[...], rows_2d(mirrored_ref[...]))
            return carry

        lax.fori_loop(0, slots // tile, rest_row, 0)

    for col in range(width // LANES):
        out_ref[:, col * capacity : (col + 1) * capacity, :] = rows_3d(
            sums[:, col * LANES : (col + 1) * LANES], capacity
        )
    counted = counted_ref[...]
    high = jnp.floor(counted * (1.0 / EXACT))
    low = counted - high * EXACT
    per_group = LANES // capacity
    extra = out_ref.shape[1] - (width // LANES) * capacity
    at_extra = (width // LANES) * capacity
    which = iota((extra, LANES), 0)
    for group in range(slots // LANES):
        both = jnp.where(
            which == 0,
            high[group : group + 1],
            jnp.where(which == 1, low[group : group + 1], 0.0),
        ).astype(jnp.bfloat16)
        out_ref[group * per_group : (group + 1) * per_group, at_extra:, :] = jnp.broadcast_to(
            both[None], (per_group, extra, LANES)
        )


def middle_kernel(
    me_ref,
    index_ref,
    arrived_ref,
    features_ref,
    cotangent_ref,
    weight_self_ref,
    weight_neigh_ref,
    bias_ref,
    output_ref,
    grad_pre_ref,
    out_ref,
):
    v_local, width = features_ref.shape
    peers = arrived_ref.shape[0]
    slots = index_ref.shape[1]
    capacity = slots // peers
    pieces = width // LANES
    index_row = index_ref[...]
    where = iota((v_local, slots), 0) == index_row
    hot = where.astype(jnp.float32).astype(jnp.bfloat16)

    extra = arrived_ref[:, pieces * capacity :, :].astype(jnp.float32)
    both = jnp.concatenate([extra[:, 0, :], extra[:, 1, :]], axis=0).astype(jnp.bfloat16)
    section = lax.rem(me_ref[0], LANES // capacity) * capacity
    place = iota((LANES, slots), 0) == section + iota((LANES, slots), 1) % capacity
    spread = dot32(both, place.astype(jnp.float32).astype(jnp.bfloat16))
    counted = diagonal_row(spread[:peers] * float(EXACT) + spread[peers:], capacity)
    degrees = jnp.sum(jnp.where(where, counted, 0.0), axis=1, keepdims=True)
    divisor = jnp.maximum(degrees, 1.0)

    sums = jnp.concatenate(
        [
            dot32(hot, rows_2d(arrived_ref[:, col * capacity : (col + 1) * capacity, :]))
            for col in range(pieces)
        ],
        axis=1,
    )
    mean_rows = (sums / divisor).astype(jnp.bfloat16)
    features = features_ref[...]
    pre_act = (
        dot32(features, weight_self_ref[...])
        + dot32(mean_rows, weight_neigh_ref[...])
        + bias_ref[...].astype(jnp.float32)
    )
    sigmoid_pre = 1.0 / (1.0 + jnp.exp(-pre_act))
    output_ref[...] = (pre_act * sigmoid_pre).astype(jnp.bfloat16)
    grad_pre32 = (
        cotangent_ref[...].astype(jnp.float32)
        * sigmoid_pre
        * (1.0 + pre_act * (1.0 - sigmoid_pre))
    )
    grad_pre = grad_pre32.astype(jnp.bfloat16)
    grad_pre_ref[...] = grad_pre
    grad_mean = (dot_general32(grad_pre, weight_neigh_ref[...], NT) / divisor).astype(jnp.bfloat16)
    outgoing = dot_general32(hot, grad_mean, TN)
    for col in range(pieces):
        out_ref[:, col * capacity : (col + 1) * capacity, :] = rows_3d(
            outgoing[:, col * LANES : (col + 1) * LANES], capacity
        )

    part_self = dot_general32(features, grad_pre, TN)
    part_neigh = dot_general32(mean_rows, grad_pre, TN)
    d_out = grad_pre.shape[1]
    share = 2 * width * (d_out // LANES) // peers
    at = pieces * capacity
    quarter = width // share
    for col in range(d_out // LANES):
        for kind, part in enumerate((part_self, part_neigh)):
            first = (col * 2 + kind) * quarter
            out_ref[first : first + quarter, at : at + share, :] = rows_3d(
                part[:, col * LANES : (col + 1) * LANES], share
            )
    part_bias = jnp.sum(grad_pre.astype(jnp.float32), axis=0, keepdims=True)
    bias_rows = out_ref.shape[1] - at - share
    which = iota((bias_rows, LANES), 0)
    high_bias = part_bias.astype(jnp.bfloat16).astype(jnp.float32)
    low_bias = part_bias - high_bias
    block = jnp.zeros((bias_rows, LANES), jnp.float32)
    for col in range(d_out // LANES):
        lanes = slice(col * LANES, (col + 1) * LANES)
        block = jnp.where(which == 2 * col, high_bias[:, lanes], block)
        block = jnp.where(which == 2 * col + 1, low_bias[:, lanes], block)
    out_ref[:, at + share :, :] = jnp.broadcast_to(
        block.astype(jnp.bfloat16)[None], (peers, bias_rows, LANES)
    )


def backward_kernel(
    norm_scale,
    capacity,
    share,
    over_ref,
    adj_t_ref,
    arrived_ref,
    rest_ref,
    out_ref,
    bias_ref,
    sums,
    stage,
    stage_sem,
):
    peers = arrived_ref.shape[0]
    tile = stage.shape[0]
    slots = peers * capacity
    pieces = sums.shape[1] // LANES
    source = jnp.concatenate(
        [
            rows_2d(arrived_ref[:, col * capacity : (col + 1) * capacity, :])
            for col in range(pieces)
        ],
        axis=1,
    )
    sums[...] = dot32(adj_t_ref[...], source)

    @pl.when(over_ref[0] != 0)
    def _():
        for row in range(slots // tile):
            rows = slice(row * tile, (row + 1) * tile)
            copy = pltpu.make_async_copy(rest_ref.at[rows], stage, stage_sem)
            copy.start()
            copy.wait()
            sums[...] += dot_general32(stage[...], source[rows], TN)

    for col in range(pieces):
        out_ref[:, col * capacity : (col + 1) * capacity, :] = rows_3d(
            sums[:, col * LANES : (col + 1) * LANES], capacity
        )
    at = pieces * capacity
    piece = jnp.sum(arrived_ref[:, at : at + share, :].astype(jnp.float32), axis=0) * norm_scale
    out_ref[:, at:, :] = jnp.broadcast_to(piece.astype(jnp.bfloat16)[None], (peers, share, LANES))
    bias = jnp.sum(arrived_ref[:, at + share :, :].astype(jnp.float32), axis=0)
    for col in range(bias_ref.shape[1] // LANES):
        bias_ref[:, col * LANES : (col + 1) * LANES] = (
            bias[2 * col : 2 * col + 1] + bias[2 * col + 1 : 2 * col + 2]
        ) * norm_scale


def end_kernel(
    index_ref, arrived_ref, grad_pre_ref, weight_self_ref, grad_x_ref, self_ref, neigh_ref
):
    v_local, width = grad_x_ref.shape
    peers = arrived_ref.shape[0]
    slots = index_ref.shape[1]
    capacity = slots // peers
    pieces = width // LANES
    hot = one_hot(index_ref[...], v_local)
    own = dot_general32(grad_pre_ref[...], weight_self_ref[...], NT)
    for col in range(pieces):
        lanes = slice(col * LANES, (col + 1) * LANES)
        back = dot32(hot, rows_2d(arrived_ref[:, col * capacity : (col + 1) * capacity, :]))
        grad_x_ref[:, lanes] = (own[:, lanes] + back).astype(jnp.bfloat16)
    at = pieces * capacity
    d_out = self_ref.shape[1]
    share = arrived_ref.shape[1] - at
    quarter = width // share
    for col in range(d_out // LANES):
        for kind, ref in enumerate((self_ref, neigh_ref)):
            first = (col * 2 + kind) * quarter
            ref[:, col * LANES : (col + 1) * LANES] = (
                arrived_ref[first : first + quarter, at:, :]
                .astype(jnp.float32)
                .reshape(width, LANES)
            )


def in_smem():
    return pl.BlockSpec(memory_space=pltpu.SMEM)


def in_vmem():
    return pl.BlockSpec(memory_space=pltpu.VMEM)


def in_place():
    return pl.BlockSpec(memory_space=pl.ANY)


def exchange(block):
    return lax.all_to_all(block, AXES, split_axis=0, concat_axis=0, tiled=True)


def per_device(
    features,
    cotangent,
    weight_self,
    weight_neigh,
    layer_bias,
    mirror_rows,
    mirror_counts,
    tile_count,
    tile_rows,
    tile_cols,
    tile_masks,
):
    f32, bf16, i32 = jnp.float32, jnp.bfloat16, jnp.int32
    v_local, width = features.shape
    d_out = weight_self.shape[1]
    peers, capacity = mirror_rows.shape[1:]
    slots = peers * capacity
    masks = tile_masks[0]
    tiles_max, tile = masks.shape[:2]
    blocks = slots // tile
    pieces = width // LANES
    share = 2 * width * (d_out // LANES) // peers
    me = lax.axis_index(AXES).astype(i32).reshape(1)
    shape = jax.ShapeDtypeStruct

    index_row, outgoing = pl.pallas_call(
        gather_kernel,
        out_shape=(shape((1, slots), i32), shape((peers, capacity, width), bf16)),
        in_specs=[in_smem(), in_vmem(), in_vmem(), in_vmem()],
        out_specs=(in_vmem(), in_vmem()),
        compiler_params=pltpu.CompilerParams(vmem_limit_bytes=16 * MIB),
        name="gather_rows",
    )(me, mirror_rows, mirror_counts, features)

    mirrored = exchange(outgoing)

    chunk, buffers = math.gcd(8, tiles_max), 8
    adj, adj_t, counted, over, rest = pl.pallas_call(
        functools.partial(build_kernel, buffers, chunk),
        out_shape=(
            shape((slots, slots), bf16),
            shape((slots, slots), bf16),
            shape((blocks, tile), f32),
            shape((1,), i32),
            shape((slots, slots), bf16),
        ),
        in_specs=[in_smem(), in_smem(), in_smem(), in_smem(), in_vmem(), in_place()],
        out_specs=(in_vmem(), in_vmem(), in_vmem(), in_smem(), in_place()),
        scratch_shapes=[
            pltpu.VMEM((blocks * blocks, tile, tile), i32),
            pltpu.VMEM((buffers, chunk, tile, tile), i32),
            pltpu.VMEM((tile, slots), bf16),
            pltpu.SemaphoreType.DMA((buffers,)),
            pltpu.SemaphoreType.DMA,
        ],
        compiler_params=pltpu.CompilerParams(vmem_limit_bytes=24 * MIB),
        cost_estimate=pl.CostEstimate(
            flops=4 * tiles_max * tile * tile,
            bytes_accessed=masks.size * 4,
            transcendentals=0,
        ),
        name="build_counts",
    )(me, tile_count, tile_rows, tile_cols, mirror_counts, masks)

    partial = pl.pallas_call(
        forward_kernel,
        out_shape=shape((peers, pieces * capacity + 8, LANES), bf16),
        in_specs=[in_smem(), in_vmem(), in_vmem(), in_vmem(), in_place()],
        out_specs=in_vmem(),
        scratch_shapes=[
            pltpu.VMEM((slots, width), f32),
            pltpu.VMEM((tile, slots), bf16),
            pltpu.SemaphoreType.DMA,
        ],
        compiler_params=pltpu.CompilerParams(vmem_limit_bytes=24 * MIB),
        name="forward_sums",
    )(over, adj, counted, mirrored, rest)

    arrived = exchange(partial)

    output, grad_pre, sent_back = pl.pallas_call(
        middle_kernel,
        out_shape=(
            shape((v_local, d_out), bf16),
            shape((v_local, d_out), bf16),
            shape((peers, pieces * capacity + share + 8, LANES), bf16),
        ),
        in_specs=[in_smem()] + [in_vmem()] * 7,
        out_specs=(in_vmem(), in_vmem(), in_vmem()),
        compiler_params=pltpu.CompilerParams(vmem_limit_bytes=24 * MIB),
        name="vertex_update",
    )(
        me,
        index_row,
        arrived,
        features,
        cotangent,
        weight_self,
        weight_neigh,
        layer_bias.reshape(1, d_out),
    )

    mirrored_grads = exchange(sent_back)

    norm_scale = 1.0 / math.sqrt(v_local * peers)
    back_partial, grad_bias = pl.pallas_call(
        functools.partial(backward_kernel, norm_scale, capacity, share),
        out_shape=(
            shape((peers, pieces * capacity + share, LANES), bf16),
            shape((1, d_out), f32),
        ),
        in_specs=[in_smem(), in_vmem(), in_vmem(), in_place()],
        out_specs=(in_vmem(), in_vmem()),
        scratch_shapes=[
            pltpu.VMEM((slots, width), f32),
            pltpu.VMEM((tile, slots), bf16),
            pltpu.SemaphoreType.DMA,
        ],
        compiler_params=pltpu.CompilerParams(vmem_limit_bytes=24 * MIB),
        name="backward_sums",
    )(over, adj_t, mirrored_grads, rest)

    back_arrived = exchange(back_partial)

    grad_x, grad_self, grad_neigh = pl.pallas_call(
        end_kernel,
        out_shape=(
            shape((v_local, width), bf16),
            shape((width, d_out), f32),
            shape((width, d_out), f32),
        ),
        in_specs=[in_vmem()] * 4,
        out_specs=(in_vmem(), in_vmem(), in_vmem()),
        compiler_params=pltpu.CompilerParams(vmem_limit_bytes=24 * MIB),
        name="vertex_grads",
    )(index_row, back_arrived, grad_pre, weight_self)

    return output, grad_x, grad_self, grad_neigh, grad_bias.reshape(d_out)


def solution(mesh):
    in_specs = (
        P(AXES, None),
        P(AXES, None),
        P(),
        P(),
        P(),
        P(AXES, None, None),
        P(),
        P(AXES),
        P(AXES, None),
        P(AXES, None),
        P(AXES, None, None, None),
    )
    out_specs = (P(AXES, None), P(AXES, None), P(), P(), P())
    return jax.shard_map(
        per_device, mesh=mesh, in_specs=in_specs, out_specs=out_specs, check_vma=False
    )
```

```python
import functools
import math

import jax
import jax.numpy as jnp
from jax import lax
from jax.experimental import pallas as pl
from jax.experimental.pallas import tpu as pltpu
from jax.sharding import PartitionSpec as P

AXES = ("grp", "dom")
LANES = 128
EXACT = 256
MIB = 1 << 20
REST_ROOM = 24
GROUP = 8

NT = (((1,), (1,)), ((), ()))
TN = (((0,), (0,)), ((), ()))


def own_index():
    return lax.axis_index(AXES)


def own_group():
    return (lax.axis_index("dom") & 1) * 4 + (lax.axis_index("grp") & 3)


def dot32(a, b):
    return jnp.dot(a, b, preferred_element_type=jnp.float32)


def dot_general32(a, b, dims):
    return lax.dot_general(a, b, dims, preferred_element_type=jnp.float32)


def iota(shape, dim):
    return lax.broadcasted_iota(jnp.int32, shape, dim)


def rows_2d(block):
    peers, rows, width = block.shape
    if rows % 16 == 0:
        return block.reshape(peers * rows, width)
    return block.astype(jnp.float32).reshape(peers * rows, width).astype(block.dtype)


def rows_3d(block, rows):
    return block.reshape(block.shape[0] // rows, rows, block.shape[1]).astype(jnp.bfloat16)


def diagonal_row(spread, capacity):
    peers, slots = spread.shape
    own = iota((peers, slots), 1) // capacity == iota((peers, slots), 0)
    return jnp.sum(jnp.where(own, spread, 0.0), axis=0, keepdims=True)


def one_hot(index_row, v_local):
    slots = index_row.shape[1]
    return (iota((v_local, slots), 0) == index_row).astype(jnp.float32).astype(jnp.bfloat16)


def gather_kernel(
    rows_hbm,
    counts_hbm,
    features_hbm,
    index_ref,
    outgoing_ref,
    rows_ref,
    counts_ref,
    features_ref,
    sems,
):
    moves = [
        pltpu.make_async_copy(source, target, sems.at[at])
        for at, (source, target) in enumerate(
            ((rows_hbm, rows_ref), (counts_hbm, counts_ref), (features_hbm, features_ref))
        )
    ]
    for move in moves:
        move.start()
    moves[0].wait()
    moves[1].wait()
    peers, capacity = rows_ref.shape[1:]
    slots = peers * capacity
    v_local = features_ref.shape[0]
    mine = iota((peers, peers), 1) == own_index()
    live_count = jnp.sum(jnp.where(mine, counts_ref[...], 0), axis=1, keepdims=True)
    live = iota((peers, capacity), 1) < live_count
    index = jnp.where(live, rows_ref[0], -1).astype(jnp.float32).astype(jnp.bfloat16)
    place = iota((capacity, slots), 1) % capacity == iota((capacity, slots), 0)
    spread = dot32(index, place.astype(jnp.float32).astype(jnp.bfloat16))
    index_row = diagonal_row(spread, capacity).astype(jnp.int32)
    index_ref[...] = index_row
    hot = one_hot(index_row, v_local)
    moves[2].wait()
    picked = dot_general32(hot, features_ref[...], TN)
    outgoing_ref[...] = rows_3d(picked, capacity)


def build_kernel(
    buffers,
    chunk,
    used_ref,
    dst_hbm,
    src_hbm,
    counts_hbm,
    masks_ref,
    adj_ref,
    counted_ref,
    over_ref,
    rest_ref,
    total,
    held,
    stage,
    dst_ref,
    src_ref,
    counts_ref,
    sems,
    stage_sem,
    small_sems,
):
    moves = [
        pltpu.make_async_copy(source, target, small_sems.at[at])
        for at, (source, target) in enumerate(
            ((dst_hbm, dst_ref), (src_hbm, src_ref), (counts_hbm, counts_ref))
        )
    ]
    for move in moves:
        move.start()
    peers = counts_ref.shape[0]
    tile = masks_ref.shape[1]
    slots = adj_ref.shape[0]
    blocks = slots // tile
    capacity = slots // peers
    used = used_ref[0]
    chunks = (used + chunk - 1) // chunk

    def fetch(step):
        slot = lax.rem(step, buffers)
        return pltpu.make_async_copy(
            masks_ref.at[pl.ds(step * chunk, chunk)], held.at[slot], sems.at[slot]
        )

    for step in range(buffers):

        @pl.when(step < chunks)
        def _():
            fetch(step).start()

    def clear(block, carry):
        total[block] = jnp.zeros((tile, tile), jnp.int32)
        return carry

    lax.fori_loop(0, blocks * blocks, clear, 0)
    for move in moves:
        move.wait()

    def one_chunk(step, carry):
        slot = lax.rem(step, buffers)
        fetch(step).wait()
        first = step * chunk

        def one_tile(at, inner):
            where = dst_ref[0, first + at] * blocks + src_ref[0, first + at]
            total[where] += held[slot, at]
            return inner

        full = first + chunk <= used

        @pl.when(full)
        def _():
            for at in range(chunk):
                one_tile(at, 0)

        @pl.when(jnp.logical_not(full))
        def _():
            lax.fori_loop(0, used - first, one_tile, 0)

        @pl.when(step + buffers < chunks)
        def _():
            fetch(step + buffers).start()

        return carry

    lax.fori_loop(0, chunks, one_chunk, 0)

    mine = iota((peers, peers), 0) == own_index()
    live_count = jnp.sum(jnp.where(mine, counts_ref[...], 0), axis=0, keepdims=True)
    live_count = jnp.broadcast_to(live_count, (8, peers)).astype(jnp.float32)
    place = iota((peers, slots), 1) // capacity == iota((peers, slots), 0)
    spread = dot32(
        live_count.astype(jnp.bfloat16), place.astype(jnp.float32).astype(jnp.bfloat16)
    )
    live_row = (iota((8, slots), 1) % capacity < spread.astype(jnp.int32)).astype(jnp.float32)

    def one_row(row, most):
        counted = jnp.zeros((tile, tile), jnp.float32)
        at_row = pl.multiple_of(row * tile, tile)
        for col in range(blocks):
            value = total[row * blocks + col]
            most = jnp.maximum(most, value)
            value = value.astype(jnp.float32)
            counted = counted + value * live_row[:1, col * tile : (col + 1) * tile]
            low = jnp.minimum(value, float(EXACT))
            adj_ref[pl.ds(at_row, tile), col * tile : (col + 1) * tile] = low.astype(jnp.bfloat16)
        counted_ref[pl.ds(row, 1), :] = jnp.sum(counted.T, axis=0, keepdims=True)
        return most

    most = lax.fori_loop(0, blocks, one_row, jnp.zeros((tile, tile), jnp.int32))
    over = jnp.max(most) > EXACT
    over_ref[0] = over.astype(jnp.int32)

    @pl.when(over)
    def _():
        def rest_row(row, carry):
            for col in range(blocks):
                value = jnp.maximum(total[row * blocks + col] - EXACT, 0)
                stage[:, col * tile : (col + 1) * tile] = value.astype(jnp.float32).astype(
                    jnp.bfloat16
                )
            copy = pltpu.make_async_copy(
                stage, rest_ref.at[pl.ds(pl.multiple_of(row * tile, tile), tile)], stage_sem
            )
            copy.start()
            copy.wait()
            return carry

        lax.fori_loop(0, blocks, rest_row, 0)


def forward_kernel(
    over_ref, adj_ref, counted_ref, mirrored_ref, rest_ref, out_ref, sums, stage, stage_sem
):
    peers, capacity, width = mirrored_ref.shape
    slots = peers * capacity
    tile = stage.shape[0]
    source = rows_2d(mirrored_ref[...])
    sums[...] = dot32(adj_ref[...], source)

    @pl.when(over_ref[0] != 0)
    def _():
        def rest_row(row, carry):
            at_row = pl.multiple_of(row * tile, tile)
            copy = pltpu.make_async_copy(rest_ref.at[pl.ds(at_row, tile)], stage, stage_sem)
            copy.start()
            copy.wait()
            sums[pl.ds(at_row, tile), :] += dot32(stage[...], rows_2d(mirrored_ref[...]))
            return carry

        lax.fori_loop(0, slots // tile, rest_row, 0)

    for col in range(width // LANES):
        out_ref[:, col * capacity : (col + 1) * capacity, :] = rows_3d(
            sums[:, col * LANES : (col + 1) * LANES], capacity
        )
    counted = counted_ref[...]
    high = jnp.floor(counted * (1.0 / EXACT))
    low = counted - high * EXACT
    per_group = LANES // capacity
    extra = out_ref.shape[1] - (width // LANES) * capacity
    at_extra = (width // LANES) * capacity
    which = iota((extra, LANES), 0)
    for group in range(slots // LANES):
        both = jnp.where(
            which == 0,
            high[group : group + 1],
            jnp.where(which == 1, low[group : group + 1], 0.0),
        ).astype(jnp.bfloat16)
        out_ref[group * per_group : (group + 1) * per_group, at_extra:, :] = jnp.broadcast_to(
            both[None], (per_group, extra, LANES)
        )


def middle_kernel(
    index_ref,
    arrived_ref,
    features_hbm,
    cotangent_hbm,
    weight_self_hbm,
    weight_neigh_hbm,
    bias_ref,
    output_ref,
    grad_pre_ref,
    out_ref,
    keep_ref,
    send_ref,
    features_ref,
    cotangent_ref,
    weight_self_ref,
    weight_neigh_ref,
    sems,
):
    moves = [
        pltpu.make_async_copy(source, target, sems.at[at])
        for at, (source, target) in enumerate(
            (
                (features_hbm, features_ref),
                (weight_self_hbm, weight_self_ref),
                (weight_neigh_hbm, weight_neigh_ref),
                (cotangent_hbm, cotangent_ref),
            )
        )
    ]
    for move in moves:
        move.start()
    v_local, width = features_ref.shape
    peers = arrived_ref.shape[0]
    slots = index_ref.shape[1]
    capacity = slots // peers
    pieces = width // LANES
    index_row = index_ref[...]
    where = iota((v_local, slots), 0) == index_row
    hot = where.astype(jnp.float32).astype(jnp.bfloat16)

    extra = arrived_ref[:, pieces * capacity :, :].astype(jnp.float32)
    both = jnp.concatenate([extra[:, 0, :], extra[:, 1, :]], axis=0).astype(jnp.bfloat16)
    section = lax.rem(own_index(), LANES // capacity) * capacity
    place = iota((LANES, slots), 0) == section + iota((LANES, slots), 1) % capacity
    spread = dot32(both, place.astype(jnp.float32).astype(jnp.bfloat16))
    counted = diagonal_row(spread[:peers] * float(EXACT) + spread[peers:], capacity)
    degrees = jnp.sum(jnp.where(where, counted, 0.0), axis=1, keepdims=True)
    divisor = jnp.maximum(degrees, 1.0)

    sums = jnp.concatenate(
        [
            dot32(hot, rows_2d(arrived_ref[:, col * capacity : (col + 1) * capacity, :]))
            for col in range(pieces)
        ],
        axis=1,
    )
    mean_rows = (sums / divisor).astype(jnp.bfloat16)
    for move in moves:
        move.wait()
    features = features_ref[...]
    weight_neigh = weight_neigh_ref[...]
    cotangent = cotangent_ref[...].astype(jnp.float32)
    pre_act = (
        dot32(features, weight_self_ref[...])
        + dot32(mean_rows, weight_neigh)
        + bias_ref[...].astype(jnp.float32)
    )
    sigmoid_pre = 1.0 / (1.0 + jnp.exp(-pre_act))
    output_ref[...] = (pre_act * sigmoid_pre).astype(jnp.bfloat16)
    grad_pre32 = (
        cotangent * sigmoid_pre * (1.0 + pre_act * (1.0 - sigmoid_pre))
    )
    grad_pre = grad_pre32.astype(jnp.bfloat16)
    grad_pre_ref[...] = grad_pre
    grad_mean = (dot_general32(grad_pre, weight_neigh, NT) / divisor).astype(jnp.bfloat16)
    out_ref[...] = rows_3d(dot_general32(hot, grad_mean, TN), capacity)

    part_self = dot_general32(features, grad_pre, TN)
    part_neigh = dot_general32(mean_rows, grad_pre, TN)
    d_out = grad_pre.shape[1]
    rows = keep_ref.shape[0]
    block = 2 * rows // GROUP
    for col in range(d_out // LANES):
        for kind, part in enumerate((part_self, part_neigh)):
            for step in range(width // block):
                number = (col * 2 + kind) * (width // block) + step
                place = number ^ own_group()
                value = part[step * block : (step + 1) * block, col * LANES : (col + 1) * LANES]

                @pl.when(place < GROUP // 2)
                def _():
                    keep_ref[pl.ds(pl.multiple_of(place * block, block), block), :] = value

                @pl.when(place >= GROUP // 2)
                def _():
                    at = pl.multiple_of((place - GROUP // 2) * block, block)
                    send_ref[pl.ds(at, block), :] = value

    part_bias = jnp.sum(grad_pre.astype(jnp.float32), axis=0, keepdims=True)
    which = iota((8, LANES), 0)
    bias_block = jnp.zeros((8, LANES), jnp.float32)
    for col in range(d_out // LANES):
        bias_block = jnp.where(
            which == col, part_bias[:, col * LANES : (col + 1) * LANES], bias_block
        )
    send_ref[rows:, :] = bias_block


def quarter_kernel(keep_ref, sent_ref, got_ref, own_ref, *other_refs):
    rows = keep_ref.shape[0]
    block = rows // 4
    for at, ref in enumerate((own_ref, *other_refs)):
        cut = slice(at * block, (at + 1) * block)
        ref[:block, :] = keep_ref[cut, :] + got_ref[cut, :]
        ref[block:, :] = sent_ref[rows:, :] + got_ref[rows:, :]


def backward_kernel(over_ref, adj_ref, arrived_ref, rest_ref, out_ref, sums, stage, stage_sem):
    peers, capacity, width = arrived_ref.shape
    tile = stage.shape[0]
    slots = peers * capacity
    source = rows_2d(arrived_ref[...])
    sums[...] = dot32(source.astype(jnp.float32).T.astype(jnp.bfloat16), adj_ref[...]).T

    @pl.when(over_ref[0] != 0)
    def _():
        for row in range(slots // tile):
            rows = slice(row * tile, (row + 1) * tile)
            copy = pltpu.make_async_copy(rest_ref.at[rows], stage, stage_sem)
            copy.start()
            copy.wait()
            sums[...] += dot_general32(stage[...], source[rows], TN)

    out_ref[...] = rows_3d(sums[...], capacity)


def end_kernel(
    norm_scale,
    index_ref,
    arrived_ref,
    grad_pre_ref,
    weight_self_ref,
    own_ref,
    near_1_ref,
    near_2_ref,
    near_3_ref,
    far_ref,
    grad_x_ref,
    self_ref,
    neigh_ref,
    bias_ref,
):
    v_local, width = grad_x_ref.shape
    capacity = arrived_ref.shape[1]
    hot = one_hot(index_ref[...], v_local)
    own = dot_general32(grad_pre_ref[...], weight_self_ref[...], NT)
    back = dot32(hot, rows_2d(arrived_ref[...]))
    grad_x_ref[...] = (own + back).astype(jnp.bfloat16)

    block = near_1_ref.shape[0]
    near_refs = (near_1_ref, near_2_ref, near_3_ref)
    d_out = self_ref.shape[1]
    per_part = width // block
    for place in range(GROUP):
        if place < 1:
            value = own_ref[:block, :]
        elif place < 4:
            value = near_refs[place - 1][...]
        else:
            value = far_ref[(place - 4) * block : (place - 3) * block, :]
        value = value * norm_scale
        number = place ^ own_group()
        at = pl.multiple_of(lax.rem(number, per_part) * block, block)
        quarter = number // per_part
        for col in range(d_out // LANES):
            for kind, ref in enumerate((self_ref, neigh_ref)):

                @pl.when(quarter == col * 2 + kind)
                def _():
                    ref[pl.ds(at, block), col * LANES : (col + 1) * LANES] = value

    for col in range(d_out // LANES):
        bias_ref[:, col * LANES : (col + 1) * LANES] = (
            own_ref[block + col : block + col + 1, :] * norm_scale
        )


def in_smem():
    return pl.BlockSpec(memory_space=pltpu.SMEM)


def in_vmem():
    return pl.BlockSpec(memory_space=pltpu.VMEM)


def in_hbm():
    return pl.BlockSpec(memory_space=pltpu.HBM)


def exchange(block):
    return lax.all_to_all(block, AXES, split_axis=0, concat_axis=0, tiled=True)


def swap(block, axis, bit):
    size = lax.axis_size(axis)
    return lax.ppermute(block, axis, [(at, at ^ bit) for at in range(size)])


def per_device(
    features,
    cotangent,
    weight_self,
    weight_neigh,
    layer_bias,
    mirror_rows,
    mirror_counts,
    tile_count,
    tile_rows,
    tile_cols,
    tile_masks,
):
    f32, bf16, i32 = jnp.float32, jnp.bfloat16, jnp.int32
    v_local, width = features.shape
    d_out = weight_self.shape[1]
    peers, capacity = mirror_rows.shape[1:]
    slots = peers * capacity
    masks = tile_masks[0]
    tiles_max, tile = masks.shape[:2]
    blocks = slots // tile
    pieces = width // LANES
    rows = 2 * width * (d_out // LANES)
    shape = jax.ShapeDtypeStruct

    index_row, outgoing = pl.pallas_call(
        gather_kernel,
        out_shape=(shape((1, slots), i32), shape((peers, capacity, width), bf16)),
        in_specs=[in_hbm()] * 3,
        out_specs=(in_vmem(), in_vmem()),
        scratch_shapes=[
            pltpu.VMEM(mirror_rows.shape, i32),
            pltpu.VMEM(mirror_counts.shape, i32),
            pltpu.VMEM(features.shape, bf16),
            pltpu.SemaphoreType.DMA((3,)),
        ],
        compiler_params=pltpu.CompilerParams(vmem_limit_bytes=60 * MIB),
        name="gather_rows",
    )(mirror_rows, mirror_counts, features)

    mirrored = exchange(outgoing)

    chunk, buffers = math.gcd(8, tiles_max), 8
    adj, counted, over, rest = pl.pallas_call(
        functools.partial(build_kernel, buffers, chunk),
        out_shape=(
            shape((slots, slots), bf16),
            shape((blocks, tile), f32),
            shape((1,), i32),
            shape((REST_ROOM * slots, slots), bf16),
        ),
        in_specs=[in_smem()] + [in_hbm()] * 4,
        out_specs=(in_vmem(), in_vmem(), in_smem(), in_hbm()),
        scratch_shapes=[
            pltpu.VMEM((blocks * blocks, tile, tile), i32),
            pltpu.VMEM((buffers, chunk, tile, tile), i32),
            pltpu.VMEM((tile, slots), bf16),
            pltpu.SMEM(tile_rows.shape, i32),
            pltpu.SMEM(tile_cols.shape, i32),
            pltpu.VMEM(mirror_counts.shape, i32),
            pltpu.SemaphoreType.DMA((buffers,)),
            pltpu.SemaphoreType.DMA,
            pltpu.SemaphoreType.DMA((3,)),
        ],
        compiler_params=pltpu.CompilerParams(vmem_limit_bytes=48 * MIB),
        cost_estimate=pl.CostEstimate(
            flops=4 * tiles_max * tile * tile,
            bytes_accessed=masks.size * 4,
            transcendentals=0,
        ),
        name="build_counts",
    )(tile_count, tile_rows, tile_cols, mirror_counts, masks)

    partial = pl.pallas_call(
        forward_kernel,
        out_shape=shape((peers, pieces * capacity + 8, LANES), bf16),
        in_specs=[in_smem(), in_vmem(), in_vmem(), in_vmem(), in_hbm()],
        out_specs=in_vmem(),
        scratch_shapes=[
            pltpu.VMEM((slots, width), f32),
            pltpu.VMEM((tile, slots), bf16),
            pltpu.SemaphoreType.DMA,
        ],
        compiler_params=pltpu.CompilerParams(vmem_limit_bytes=24 * MIB),
        name="forward_sums",
    )(over, adj, counted, mirrored, rest)

    arrived = exchange(partial)

    output, grad_pre, sent_back, keep, send = pl.pallas_call(
        middle_kernel,
        out_shape=(
            shape((v_local, d_out), bf16),
            shape((v_local, d_out), bf16),
            shape((peers, capacity, width), bf16),
            shape((rows // 2, LANES), f32),
            shape((rows // 2 + 8, LANES), f32),
        ),
        in_specs=[in_vmem()] * 2 + [in_hbm()] * 4 + [in_vmem()],
        out_specs=(in_vmem(),) * 5,
        scratch_shapes=[
            pltpu.VMEM(features.shape, bf16),
            pltpu.VMEM(cotangent.shape, bf16),
            pltpu.VMEM(weight_self.shape, bf16),
            pltpu.VMEM(weight_neigh.shape, bf16),
            pltpu.SemaphoreType.DMA((4,)),
        ],
        compiler_params=pltpu.CompilerParams(vmem_limit_bytes=8 * MIB),
        name="vertex_update",
    )(
        index_row,
        arrived,
        features,
        cotangent,
        weight_self,
        weight_neigh,
        layer_bias.reshape(1, d_out),
    )

    mirrored_grads = exchange(sent_back)

    got = swap(send, "dom", 1)
    half, quarter = rows // 2, rows // GROUP
    summed = keep + got[:half]
    bias_sum = send[half:] + got[half:]
    own, *others = [
        jnp.concatenate([summed[at * quarter : (at + 1) * quarter], bias_sum]) for at in range(4)
    ]
    got = [swap(other, "grp", bit) for bit, other in zip((1, 2, 3), others, strict=True)]
    full = (own + got[0]) + (got[1] + got[2])
    bit = 2
    while bit < lax.axis_size("dom"):
        sent = full.astype(bf16)
        got = [
            swap(sent, "dom", other)
            for other in (bit, 2 * bit, 3 * bit)
            if other < lax.axis_size("dom")
        ]
        wide = [value.astype(f32) for value in (sent, *got)]
        full = wide[0] + wide[1]
        if len(wide) == 4:
            full = full + (wide[2] + wide[3])
        bit *= 4
    full, mirrored_grads = lax.optimization_barrier((full, mirrored_grads))
    block = full[: rows // GROUP]
    near = [swap(block, "grp", bit) for bit in (1, 2, 3)]
    far = swap(jnp.concatenate([block, *near]), "dom", 1)

    back_partial = pl.pallas_call(
        backward_kernel,
        out_shape=shape((peers, capacity, width), bf16),
        in_specs=[in_smem(), in_vmem(), in_vmem(), in_hbm()],
        out_specs=in_vmem(),
        scratch_shapes=[
            pltpu.VMEM((slots, width), f32),
            pltpu.VMEM((tile, slots), bf16),
            pltpu.SemaphoreType.DMA,
        ],
        compiler_params=pltpu.CompilerParams(vmem_limit_bytes=24 * MIB),
        name="backward_sums",
    )(over, adj, mirrored_grads, rest)

    back_arrived = exchange(back_partial)

    norm_scale = 1.0 / math.sqrt(v_local * peers)
    grad_x, grad_self, grad_neigh, grad_bias = pl.pallas_call(
        functools.partial(end_kernel, norm_scale),
        out_shape=(
            shape((v_local, width), bf16),
            shape((width, d_out), f32),
            shape((width, d_out), f32),
            shape((1, d_out), f32),
        ),
        in_specs=[in_vmem()] * 9,
        out_specs=(in_vmem(),) * 4,
        compiler_params=pltpu.CompilerParams(vmem_limit_bytes=8 * MIB),
        name="vertex_grads",
    )(index_row, back_arrived, grad_pre, weight_self, full, *near, far)

    return output, grad_x, grad_self, grad_neigh, grad_bias.reshape(d_out)


def solution(mesh):
    in_specs = (
        P(AXES, None),
        P(AXES, None),
        P(),
        P(),
        P(),
        P(AXES, None, None),
        P(),
        P(AXES),
        P(AXES, None),
        P(AXES, None),
        P(AXES, None, None, None),
    )
    out_specs = (P(AXES, None), P(AXES, None), P(), P(), P())
    return jax.shard_map(
        per_device, mesh=mesh, in_specs=in_specs, out_specs=out_specs, check_vma=False
    )
```

```python
import functools
import math

import jax
import jax.numpy as jnp
from jax import lax
from jax.experimental import pallas as pl
from jax.experimental.pallas import tpu as pltpu
from jax.sharding import PartitionSpec as P

AXES = ("grp", "dom")
LANES = 128
EXACT = 256
MIB = 1 << 20
PIECES = 4
REST_ROOM = 24
GROUP = 8

NT = (((1,), (1,)), ((), ()))
TN = (((0,), (0,)), ((), ()))


def own_index():
    return lax.axis_index(AXES)


def own_group():
    return (lax.axis_index("dom") & 1) * 4 + (lax.axis_index("grp") & 3)


def dot32(a, b):
    return jnp.dot(a, b, preferred_element_type=jnp.float32)


def dot_general32(a, b, dims):
    return lax.dot_general(a, b, dims, preferred_element_type=jnp.float32)


def iota(shape, dim):
    return lax.broadcasted_iota(jnp.int32, shape, dim)


def rows_2d(block):
    peers, rows, width = block.shape
    if rows % 16 == 0:
        return block.reshape(peers * rows, width)
    return block.astype(jnp.float32).reshape(peers * rows, width).astype(block.dtype)


def rows_3d(block, rows):
    return block.reshape(block.shape[0] // rows, rows, block.shape[1]).astype(jnp.bfloat16)


class Pieces:
    def __init__(self, stage, target, sems, capacity):
        self.capacity = capacity
        self.stage, self.target, self.sems = stage, target, sems
        self.count = sems.shape[0]
        self.peers = stage.shape[0] // self.count
        self.copies = []

    def rows(self, piece):
        return slice(piece * self.peers, (piece + 1) * self.peers)

    def slots(self, piece):
        per_piece = self.peers * self.capacity
        return slice(piece * per_piece, (piece + 1) * per_piece)

    def start(self, piece):
        copy = pltpu.make_async_copy(
            self.stage.at[self.rows(piece)], self.target.at[self.rows(piece)], self.sems.at[piece]
        )
        copy.start()
        self.copies.append(copy)

    def send(self, piece, value):
        self.stage[self.rows(piece)] = value
        self.start(piece)

    def wait(self):
        for copy in self.copies:
            copy.wait()


def diagonal_row(spread, capacity):
    peers, slots = spread.shape
    own = iota((peers, slots), 1) // capacity == iota((peers, slots), 0)
    return jnp.sum(jnp.where(own, spread, 0.0), axis=0, keepdims=True)


def one_hot(index_row, v_local):
    slots = index_row.shape[1]
    return (iota((v_local, slots), 0) == index_row).astype(jnp.float32).astype(jnp.bfloat16)


def gather_kernel(
    rows_hbm,
    counts_hbm,
    features_hbm,
    index_ref,
    outgoing_ref,
    rows_ref,
    counts_ref,
    features_ref,
    sems,
):
    moves = [
        pltpu.make_async_copy(source, target, sems.at[at])
        for at, (source, target) in enumerate(
            ((rows_hbm, rows_ref), (counts_hbm, counts_ref), (features_hbm, features_ref))
        )
    ]
    for move in moves:
        move.start()
    moves[0].wait()
    moves[1].wait()
    peers, capacity = rows_ref.shape[1:]
    slots = peers * capacity
    v_local = features_ref.shape[0]
    mine = iota((peers, peers), 1) == own_index()
    live_count = jnp.sum(jnp.where(mine, counts_ref[...], 0), axis=1, keepdims=True)
    live = iota((peers, capacity), 1) < live_count
    index = jnp.where(live, rows_ref[0], -1).astype(jnp.float32).astype(jnp.bfloat16)
    place = iota((capacity, slots), 1) % capacity == iota((capacity, slots), 0)
    spread = dot32(index, place.astype(jnp.float32).astype(jnp.bfloat16))
    index_row = diagonal_row(spread, capacity).astype(jnp.int32)
    index_ref[...] = index_row
    hot = one_hot(index_row, v_local)
    moves[2].wait()
    picked = dot_general32(hot, features_ref[...], TN)
    outgoing_ref[...] = rows_3d(picked, capacity)


def build_kernel(
    buffers,
    chunk,
    used_ref,
    dst_hbm,
    src_hbm,
    counts_hbm,
    masks_ref,
    adj_ref,
    counted_ref,
    rest_ref,
    total,
    held,
    stage,
    dst_ref,
    src_ref,
    counts_ref,
    sems,
    stage_sem,
    small_sems,
):
    moves = [
        pltpu.make_async_copy(source, target, small_sems.at[at])
        for at, (source, target) in enumerate(
            ((dst_hbm, dst_ref), (src_hbm, src_ref), (counts_hbm, counts_ref))
        )
    ]
    for move in moves:
        move.start()
    peers = counts_ref.shape[0]
    tile = masks_ref.shape[1]
    slots = adj_ref.shape[0]
    blocks = slots // tile
    capacity = slots // peers
    used = used_ref[0]
    chunks = (used + chunk - 1) // chunk

    def fetch(step):
        slot = lax.rem(step, buffers)
        return pltpu.make_async_copy(
            masks_ref.at[pl.ds(step * chunk, chunk)], held.at[slot], sems.at[slot]
        )

    for step in range(buffers):

        @pl.when(step < chunks)
        def _():
            fetch(step).start()

    def clear(block, carry):
        total[block] = jnp.zeros((tile, tile), jnp.int32)
        return carry

    lax.fori_loop(0, blocks * blocks, clear, 0)
    for move in moves:
        move.wait()

    def one_chunk(step, carry):
        slot = lax.rem(step, buffers)
        fetch(step).wait()
        first = step * chunk

        def one_tile(at, inner):
            where = dst_ref[0, first + at] * blocks + src_ref[0, first + at]
            total[where] += held[slot, at]
            return inner

        full = first + chunk <= used

        @pl.when(full)
        def _():
            for at in range(chunk):
                one_tile(at, 0)

        @pl.when(jnp.logical_not(full))
        def _():
            lax.fori_loop(0, used - first, one_tile, 0)

        @pl.when(step + buffers < chunks)
        def _():
            fetch(step + buffers).start()

        return carry

    lax.fori_loop(0, chunks, one_chunk, 0)

    mine = iota((peers, peers), 0) == own_index()
    live_count = jnp.sum(jnp.where(mine, counts_ref[...], 0), axis=0, keepdims=True)
    live_count = jnp.broadcast_to(live_count, (8, peers)).astype(jnp.float32)
    place = iota((peers, slots), 1) // capacity == iota((peers, slots), 0)
    spread = dot32(
        live_count.astype(jnp.bfloat16), place.astype(jnp.float32).astype(jnp.bfloat16)
    )
    live_row = (iota((8, slots), 1) % capacity < spread.astype(jnp.int32)).astype(jnp.float32)

    def one_row(row, most):
        counted = jnp.zeros((tile, tile), jnp.float32)
        at_row = pl.multiple_of(row * tile, tile)
        for col in range(blocks):
            value = total[row * blocks + col]
            most = jnp.maximum(most, value)
            value = value.astype(jnp.float32)
            counted = counted + value * live_row[:1, col * tile : (col + 1) * tile]
            low = jnp.minimum(value, float(EXACT))
            adj_ref[pl.ds(at_row, tile), col * tile : (col + 1) * tile] = low.astype(jnp.bfloat16)
        counted_ref[pl.ds(row, 1), :] = jnp.sum(counted.T, axis=0, keepdims=True)
        return most

    most = lax.fori_loop(0, blocks, one_row, jnp.zeros((tile, tile), jnp.int32))
    over = jnp.max(most) > EXACT
    counted_ref[blocks:, :] = jnp.full((8, tile), over.astype(jnp.float32))

    @pl.when(over)
    def _():
        def rest_row(row, carry):
            for col in range(blocks):
                value = jnp.maximum(total[row * blocks + col] - EXACT, 0)
                stage[:, col * tile : (col + 1) * tile] = value.astype(jnp.float32).astype(
                    jnp.bfloat16
                )
            copy = pltpu.make_async_copy(
                stage, rest_ref.at[pl.ds(pl.multiple_of(row * tile, tile), tile)], stage_sem
            )
            copy.start()
            copy.wait()
            return carry

        lax.fori_loop(0, blocks, rest_row, 0)


def forward_kernel(
    adj_ref,
    counted_ref,
    mirrored_ref,
    rest_ref,
    out_hbm,
    out_ref,
    more,
    stage,
    stage_sem,
    sems,
):
    peers, capacity, width = mirrored_ref.shape
    slots = peers * capacity
    tile = stage.shape[0]
    columns = width // LANES
    source = rows_2d(mirrored_ref[...])
    counted = counted_ref[: slots // tile, :]
    over = jnp.max(counted_ref[slots // tile :, :]) > 0
    high = jnp.floor(counted * (1.0 / EXACT))
    low = counted - high * EXACT
    per_group = LANES // capacity
    at_extra = columns * capacity
    extra = out_ref.shape[1] - at_extra
    which = iota((extra, LANES), 0)
    for group in range(slots // LANES):
        both = jnp.where(
            which == 0,
            high[group : group + 1],
            jnp.where(which == 1, low[group : group + 1], 0.0),
        ).astype(jnp.bfloat16)
        out_ref[group * per_group : (group + 1) * per_group, at_extra:, :] = jnp.broadcast_to(
            both[None], (per_group, extra, LANES)
        )

    def multiply(add_rest):
        pieces = Pieces(out_ref, out_hbm, sems, capacity)
        for piece in range(pieces.count):
            sums = dot32(adj_ref[pieces.slots(piece), :], source)
            if add_rest:
                sums += more[pieces.slots(piece), :]
            for col in range(columns):
                out_ref[pieces.rows(piece), col * capacity : (col + 1) * capacity, :] = rows_3d(
                    sums[:, col * LANES : (col + 1) * LANES], capacity
                )
            pieces.start(piece)
        pieces.wait()

    @pl.when(jnp.logical_not(over))
    def _():
        multiply(False)

    @pl.when(over)
    def _():
        for row in range(slots // tile):
            rows = slice(row * tile, (row + 1) * tile)
            copy = pltpu.make_async_copy(rest_ref.at[rows], stage, stage_sem)
            copy.start()
            copy.wait()
            more[rows, :] = dot32(stage[...], source)
        multiply(True)


def middle_kernel(
    index_ref,
    arrived_ref,
    features_ref,
    cotangent_ref,
    weight_self_ref,
    weight_neigh_ref,
    bias_ref,
    output_hbm,
    mean_hbm,
    grad_pre_hbm,
    out_hbm,
    output_ref,
    mean_ref,
    grad_pre_ref,
    stage,
    result_sems,
    out_sems,
):
    v_local, width = features_ref.shape
    peers = arrived_ref.shape[0]
    slots = index_ref.shape[1]
    capacity = slots // peers
    columns = width // LANES
    where = iota((v_local, slots), 0) == index_ref[...]
    hot = where.astype(jnp.float32).astype(jnp.bfloat16)

    extra = arrived_ref[:, columns * capacity :, :].astype(jnp.float32)
    both = jnp.concatenate([extra[:, 0, :], extra[:, 1, :]], axis=0).astype(jnp.bfloat16)
    section = lax.rem(own_index(), LANES // capacity) * capacity
    place = iota((LANES, slots), 0) == section + iota((LANES, slots), 1) % capacity
    spread = dot32(both, place.astype(jnp.float32).astype(jnp.bfloat16))
    counted = diagonal_row(spread[:peers] * float(EXACT) + spread[peers:], capacity)
    degrees = jnp.sum(jnp.where(where, counted, 0.0), axis=1, keepdims=True)
    divisor = jnp.maximum(degrees, 1.0)

    partial = jnp.concatenate(
        [
            rows_2d(arrived_ref[:, col * capacity : (col + 1) * capacity, :])
            for col in range(columns)
        ],
        axis=1,
    )
    mean_rows = (dot32(hot, partial) / divisor).astype(jnp.bfloat16)
    mean_ref[...] = mean_rows
    pre_act = (
        dot32(features_ref[...], weight_self_ref[...])
        + dot32(mean_rows, weight_neigh_ref[...])
        + bias_ref[...].astype(jnp.float32)
    )
    sigmoid_pre = 1.0 / (1.0 + jnp.exp(-pre_act))
    grad_pre32 = (
        cotangent_ref[...].astype(jnp.float32)
        * sigmoid_pre
        * (1.0 + pre_act * (1.0 - sigmoid_pre))
    )
    grad_pre = grad_pre32.astype(jnp.bfloat16)
    grad_mean = (dot_general32(grad_pre, weight_neigh_ref[...], NT) / divisor).astype(jnp.bfloat16)
    pieces = Pieces(stage, out_hbm, out_sems, capacity)
    for piece in range(pieces.count):
        picked = dot_general32(hot[:, pieces.slots(piece)], grad_mean, TN)
        pieces.send(piece, rows_3d(picked, capacity))
    grad_pre_ref[...] = grad_pre
    output_ref[...] = (pre_act * sigmoid_pre).astype(jnp.bfloat16)
    results = [
        pltpu.make_async_copy(source, target, result_sems.at[at])
        for at, (source, target) in enumerate(
            ((mean_ref, mean_hbm), (grad_pre_ref, grad_pre_hbm), (output_ref, output_hbm))
        )
    ]
    for result in results:
        result.start()
    pieces.wait()
    for result in results:
        result.wait()


def parts_kernel(features_ref, mean_ref, grad_pre_ref, keep_ref, send_ref):
    grad_pre = grad_pre_ref[...]
    width, d_out = features_ref.shape[1], grad_pre.shape[1]
    rows = keep_ref.shape[0]
    block = 2 * rows // GROUP
    for kind, rows_ref in enumerate((features_ref, mean_ref)):
        part = dot_general32(rows_ref[...], grad_pre, TN)
        for col in range(d_out // LANES):
            for step in range(width // block):
                number = (col * 2 + kind) * (width // block) + step
                place = number ^ own_group()
                value = part[step * block : (step + 1) * block, col * LANES : (col + 1) * LANES]

                @pl.when(place < GROUP // 2)
                def _():
                    keep_ref[pl.ds(pl.multiple_of(place * block, block), block), :] = value

                @pl.when(place >= GROUP // 2)
                def _():
                    at = pl.multiple_of((place - GROUP // 2) * block, block)
                    send_ref[pl.ds(at, block), :] = value

    part_bias = jnp.sum(grad_pre.astype(jnp.float32), axis=0, keepdims=True)
    which = iota((8, LANES), 0)
    bias_block = jnp.zeros((8, LANES), jnp.float32)
    for col in range(d_out // LANES):
        bias_block = jnp.where(
            which == col, part_bias[:, col * LANES : (col + 1) * LANES], bias_block
        )
    send_ref[rows:, :] = bias_block


def quarter_kernel(keep_ref, sent_ref, got_ref, own_ref, *other_refs):
    rows = keep_ref.shape[0]
    block = rows // 4
    for at, ref in enumerate((own_ref, *other_refs)):
        cut = slice(at * block, (at + 1) * block)
        ref[:block, :] = (keep_ref[cut, :] + got_ref[cut, :]).astype(ref.dtype)
        ref[block:, :] = (sent_ref[rows:, :] + got_ref[rows:, :]).astype(ref.dtype)


def backward_kernel(
    adj_ref, counted_ref, arrived_ref, rest_ref, out_hbm, out_ref, more, stage, stage_sem, sems
):
    peers, capacity, width = arrived_ref.shape
    tile = stage.shape[0]
    slots = peers * capacity
    source = rows_2d(arrived_ref[...])
    over = jnp.max(counted_ref[slots // tile :, :]) > 0
    source_t = source.astype(jnp.float32).T.astype(jnp.bfloat16)

    def multiply(add_rest):
        pieces = Pieces(out_ref, out_hbm, sems, capacity)
        for piece in range(pieces.count):
            sums = dot32(source_t, adj_ref[:, pieces.slots(piece)]).T
            if add_rest:
                sums += more[pieces.slots(piece), :]
            pieces.send(piece, rows_3d(sums, capacity))
        pieces.wait()

    @pl.when(jnp.logical_not(over))
    def _():
        multiply(False)

    @pl.when(over)
    def _():
        more[...] = jnp.zeros_like(more)
        for row in range(slots // tile):
            rows = slice(row * tile, (row + 1) * tile)
            copy = pltpu.make_async_copy(rest_ref.at[rows], stage, stage_sem)
            copy.start()
            copy.wait()
            more[...] += dot_general32(stage[...], source[rows], TN)
        multiply(True)


def layout_kernel(
    norm_scale,
    own_ref,
    near_1_ref,
    near_2_ref,
    near_3_ref,
    far_ref,
    self_ref,
    neigh_ref,
    bias_ref,
):
    block = near_1_ref.shape[0]
    near_refs = (near_1_ref, near_2_ref, near_3_ref)
    width, d_out = self_ref.shape
    per_part = width // block
    for place in range(GROUP):
        if place < 1:
            value = own_ref[:block, :]
        elif place < 4:
            value = near_refs[place - 1][...]
        else:
            value = far_ref[(place - 4) * block : (place - 3) * block, :]
        value = value.astype(jnp.float32) * norm_scale
        number = place ^ own_group()
        at = pl.multiple_of(lax.rem(number, per_part) * block, block)
        quarter = number // per_part
        for col in range(d_out // LANES):
            for kind, ref in enumerate((self_ref, neigh_ref)):

                @pl.when(quarter == col * 2 + kind)
                def _():
                    ref[pl.ds(at, block), col * LANES : (col + 1) * LANES] = value

    for col in range(d_out // LANES):
        bias_ref[:, col * LANES : (col + 1) * LANES] = (
            own_ref[block + col : block + col + 1, :].astype(jnp.float32) * norm_scale
        )


def end_kernel(index_ref, arrived_ref, grad_pre_ref, weight_self_ref, grad_x_ref):
    v_local = grad_x_ref.shape[0]
    hot = one_hot(index_ref[...], v_local)
    own = dot_general32(grad_pre_ref[...], weight_self_ref[...], NT)
    back = dot32(hot, rows_2d(arrived_ref[...]))
    grad_x_ref[...] = (own + back).astype(jnp.bfloat16)


def in_smem():
    return pl.BlockSpec(memory_space=pltpu.SMEM)


def in_vmem():
    return pl.BlockSpec(memory_space=pltpu.VMEM)


def in_hbm():
    return pl.BlockSpec(memory_space=pltpu.HBM)


def exchange(block):
    return lax.all_to_all(block, AXES, split_axis=0, concat_axis=0, tiled=True)


def swap(block, axis, bit):
    size = lax.axis_size(axis)
    return lax.ppermute(block, axis, [(at, at ^ bit) for at in range(size)])


def per_device(
    features,
    cotangent,
    weight_self,
    weight_neigh,
    layer_bias,
    mirror_rows,
    mirror_counts,
    tile_count,
    tile_rows,
    tile_cols,
    tile_masks,
):
    f32, bf16, i32 = jnp.float32, jnp.bfloat16, jnp.int32
    v_local, width = features.shape
    d_out = weight_self.shape[1]
    peers, capacity = mirror_rows.shape[1:]
    slots = peers * capacity
    masks = tile_masks[0]
    tiles_max, tile = masks.shape[:2]
    blocks = slots // tile
    pieces = width // LANES
    rows = 2 * width * (d_out // LANES)
    shape = jax.ShapeDtypeStruct

    index_row, outgoing = pl.pallas_call(
        gather_kernel,
        out_shape=(shape((1, slots), i32), shape((peers, capacity, width), bf16)),
        in_specs=[in_hbm()] * 3,
        out_specs=(in_vmem(), in_vmem()),
        scratch_shapes=[
            pltpu.VMEM(mirror_rows.shape, i32),
            pltpu.VMEM(mirror_counts.shape, i32),
            pltpu.VMEM(features.shape, bf16),
            pltpu.SemaphoreType.DMA((3,)),
        ],
        compiler_params=pltpu.CompilerParams(vmem_limit_bytes=60 * MIB),
        name="gather_rows",
    )(mirror_rows, mirror_counts, features)

    mirrored = exchange(outgoing)

    chunk, buffers = math.gcd(8, tiles_max), 8
    adj, counted, rest = pl.pallas_call(
        functools.partial(build_kernel, buffers, chunk),
        out_shape=(
            shape((slots, slots), bf16),
            shape((blocks + 8, tile), f32),
            shape((REST_ROOM * slots, slots), bf16),
        ),
        in_specs=[in_smem()] + [in_hbm()] * 4,
        out_specs=(in_vmem(), in_vmem(), in_hbm()),
        scratch_shapes=[
            pltpu.VMEM((blocks * blocks, tile, tile), i32),
            pltpu.VMEM((buffers, chunk, tile, tile), i32),
            pltpu.VMEM((tile, slots), bf16),
            pltpu.SMEM(tile_rows.shape, i32),
            pltpu.SMEM(tile_cols.shape, i32),
            pltpu.VMEM(mirror_counts.shape, i32),
            pltpu.SemaphoreType.DMA((buffers,)),
            pltpu.SemaphoreType.DMA,
            pltpu.SemaphoreType.DMA((3,)),
        ],
        compiler_params=pltpu.CompilerParams(vmem_limit_bytes=48 * MIB),
        cost_estimate=pl.CostEstimate(
            flops=4 * tiles_max * tile * tile,
            bytes_accessed=masks.size * 4,
            transcendentals=0,
        ),
        name="build_counts",
    )(tile_count, tile_rows, tile_cols, mirror_counts, masks)

    partial_shape = (peers, pieces * capacity + 8, LANES)
    partial = pl.pallas_call(
        forward_kernel,
        out_shape=shape(partial_shape, bf16),
        in_specs=[in_vmem(), in_vmem(), in_vmem(), in_hbm()],
        out_specs=in_hbm(),
        scratch_shapes=[
            pltpu.VMEM(partial_shape, bf16),
            pltpu.VMEM((slots, width), f32),
            pltpu.VMEM((tile, slots), bf16),
            pltpu.SemaphoreType.DMA,
            pltpu.SemaphoreType.DMA((PIECES,)),
        ],
        compiler_params=pltpu.CompilerParams(vmem_limit_bytes=8 * MIB),
        name="forward_sums",
    )(adj, counted, mirrored, rest)

    arrived = exchange(partial)

    output, mean_rows, grad_pre, sent_back = pl.pallas_call(
        middle_kernel,
        out_shape=(
            shape((v_local, d_out), bf16),
            shape((v_local, width), bf16),
            shape((v_local, d_out), bf16),
            shape((peers, capacity, width), bf16),
        ),
        in_specs=[in_vmem()] * 7,
        out_specs=(in_hbm(),) * 4,
        scratch_shapes=[
            pltpu.VMEM((v_local, d_out), bf16),
            pltpu.VMEM((v_local, width), bf16),
            pltpu.VMEM((v_local, d_out), bf16),
            pltpu.VMEM((peers, capacity, width), bf16),
            pltpu.SemaphoreType.DMA((3,)),
            pltpu.SemaphoreType.DMA((PIECES,)),
        ],
        compiler_params=pltpu.CompilerParams(vmem_limit_bytes=8 * MIB),
        name="vertex_update",
    )(
        index_row,
        arrived,
        features,
        cotangent,
        weight_self,
        weight_neigh,
        layer_bias.reshape(1, d_out),
    )

    mirrored_grads = exchange(sent_back)

    keep, send = pl.pallas_call(
        parts_kernel,
        out_shape=(
            shape((rows // 2, LANES), f32),
            shape((rows // 2 + 8, LANES), f32),
        ),
        in_specs=[in_vmem()] * 3,
        out_specs=(in_vmem(),) * 2,
        compiler_params=pltpu.CompilerParams(vmem_limit_bytes=24 * MIB),
        cost_estimate=pl.CostEstimate(flops=1 << 27, bytes_accessed=1 << 20, transcendentals=0),
        name="weight_parts",
    )(features, mean_rows, grad_pre)

    got = swap(send, "dom", 1)
    own, *others = pl.pallas_call(
        quarter_kernel,
        out_shape=tuple(shape((rows // GROUP + 8, LANES), kind) for kind in (f32, bf16, bf16, bf16)),
        in_specs=[in_vmem()] * 3,
        out_specs=(in_vmem(),) * 4,
        compiler_params=pltpu.CompilerParams(vmem_limit_bytes=2 * MIB),
        name="quarter_sums",
    )(keep, send, got)
    got = [swap(other, "grp", bit) for bit, other in zip((1, 2, 3), others, strict=True)]
    full = (own + got[0].astype(f32)) + (got[1].astype(f32) + got[2].astype(f32))
    bit = 2
    while bit < lax.axis_size("dom"):
        sent = full.astype(bf16)
        got = [
            swap(sent, "dom", other)
            for other in (bit, 2 * bit, 3 * bit)
            if other < lax.axis_size("dom")
        ]
        wide = [value.astype(f32) for value in (sent, *got)]
        full = wide[0] + wide[1]
        if len(wide) == 4:
            full = full + (wide[2] + wide[3])
        bit *= 4
    full, mirrored_grads = lax.optimization_barrier((full, mirrored_grads))
    back_partial = pl.pallas_call(
        backward_kernel,
        out_shape=shape((peers, capacity, width), bf16),
        in_specs=[in_vmem(), in_vmem(), in_vmem(), in_hbm()],
        out_specs=in_hbm(),
        scratch_shapes=[
            pltpu.VMEM((peers, capacity, width), bf16),
            pltpu.VMEM((slots, width), f32),
            pltpu.VMEM((tile, slots), bf16),
            pltpu.SemaphoreType.DMA,
            pltpu.SemaphoreType.DMA((PIECES,)),
        ],
        compiler_params=pltpu.CompilerParams(vmem_limit_bytes=32 * MIB),
        cost_estimate=pl.CostEstimate(flops=1 << 29, bytes_accessed=3 << 20, transcendentals=0),
        name="backward_sums",
    )(adj, counted, mirrored_grads, rest)

    back_arrived = exchange(back_partial)

    full = full.astype(bf16)
    block = full[: rows // GROUP]
    near = [swap(block, "grp", bit) for bit in (1, 2, 3)]
    far = swap(jnp.concatenate([block, *near]), "dom", 1)

    norm_scale = 1.0 / math.sqrt(v_local * peers)
    grad_self, grad_neigh, grad_bias = pl.pallas_call(
        functools.partial(layout_kernel, norm_scale),
        out_shape=(
            shape((width, d_out), f32),
            shape((width, d_out), f32),
            shape((1, d_out), f32),
        ),
        in_specs=[in_vmem()] * 5,
        out_specs=(in_vmem(),) * 3,
        compiler_params=pltpu.CompilerParams(vmem_limit_bytes=2 * MIB),
        name="weight_layout",
    )(full, *near, far)

    grad_x = pl.pallas_call(
        end_kernel,
        out_shape=shape((v_local, width), bf16),
        in_specs=[in_vmem()] * 4,
        out_specs=in_vmem(),
        compiler_params=pltpu.CompilerParams(vmem_limit_bytes=4 * MIB),
        name="vertex_grads",
    )(index_row, back_arrived, grad_pre, weight_self)

    return output, grad_x, grad_self, grad_neigh, grad_bias.reshape(d_out)


def solution(mesh):
    in_specs = (
        P(AXES, None),
        P(AXES, None),
        P(),
        P(),
        P(),
        P(AXES, None, None),
        P(),
        P(AXES),
        P(AXES, None),
        P(AXES, None),
        P(AXES, None, None, None),
    )
    out_specs = (P(AXES, None), P(AXES, None), P(), P(), P())
    return jax.shard_map(
        per_device, mesh=mesh, in_specs=in_specs, out_specs=out_specs, check_vma=False
    )
```

```python
import functools
import math

import jax
import jax.numpy as jnp
from jax import lax
from jax.experimental import pallas as pl
from jax.experimental.pallas import tpu as pltpu
from jax.sharding import PartitionSpec as P

AXES = ("grp", "dom")
LANES = 128
EXACT = 256
MIB = 1 << 20
PIECES = 4
REST_ROOM = 24
GROUP = 8

NT = (((1,), (1,)), ((), ()))
TN = (((0,), (0,)), ((), ()))


def own_index():
    return lax.axis_index(AXES)


def own_group():
    return (lax.axis_index("dom") & 1) * 4 + (lax.axis_index("grp") & 3)


def dot32(a, b):
    return jnp.dot(a, b, preferred_element_type=jnp.float32)


def dot_general32(a, b, dims):
    return lax.dot_general(a, b, dims, preferred_element_type=jnp.float32)


def iota(shape, dim):
    return lax.broadcasted_iota(jnp.int32, shape, dim)


def rows_2d(block):
    peers, rows, width = block.shape
    if rows % 16 == 0:
        return block.reshape(peers * rows, width)
    return block.astype(jnp.float32).reshape(peers * rows, width).astype(block.dtype)


def rows_3d(block, rows):
    return block.reshape(block.shape[0] // rows, rows, block.shape[1]).astype(jnp.bfloat16)


class Pieces:
    def __init__(self, stage, target, sems, capacity):
        self.capacity = capacity
        self.stage, self.target, self.sems = stage, target, sems
        self.count = sems.shape[0]
        self.peers = stage.shape[0] // self.count
        self.copies = []

    def rows(self, piece):
        return slice(piece * self.peers, (piece + 1) * self.peers)

    def slots(self, piece):
        per_piece = self.peers * self.capacity
        return slice(piece * per_piece, (piece + 1) * per_piece)

    def start(self, piece):
        copy = pltpu.make_async_copy(
            self.stage.at[self.rows(piece)], self.target.at[self.rows(piece)], self.sems.at[piece]
        )
        copy.start()
        self.copies.append(copy)

    def send(self, piece, value):
        self.stage[self.rows(piece)] = value
        self.start(piece)

    def wait(self):
        for copy in self.copies:
            copy.wait()


def diagonal_row(spread, capacity):
    peers, slots = spread.shape
    own = iota((peers, slots), 1) // capacity == iota((peers, slots), 0)
    return jnp.sum(jnp.where(own, spread, 0.0), axis=0, keepdims=True)


def ones(mask):
    return mask.astype(jnp.float32).astype(jnp.bfloat16)


def one_hot(index_row, v_local):
    return ones(iota((v_local, index_row.shape[1]), 0) == index_row)


def as_column(index, slots):
    peers, capacity = index.shape
    spread = dot32(ones(iota((slots, peers), 0) // capacity == iota((slots, peers), 1)), index)
    own = iota((slots, capacity), 0) % capacity == iota((slots, capacity), 1)
    return jnp.sum(jnp.where(own, spread, 0.0), axis=1, keepdims=True).astype(jnp.int32)


def as_row(index, slots):
    capacity = index.shape[1]
    place = ones(iota((capacity, slots), 1) % capacity == iota((capacity, slots), 0))
    return diagonal_row(dot32(index, place), capacity).astype(jnp.int32)


def gather_kernel(
    rows_hbm,
    counts_hbm,
    features_hbm,
    dst_hbm,
    src_hbm,
    facts_ref,
    outgoing_ref,
    rows_ref,
    counts_ref,
    features_ref,
    dst_ref,
    src_ref,
    sems,
):
    moves = [
        pltpu.make_async_copy(source, target, sems.at[at])
        for at, (source, target) in enumerate(
            (
                (rows_hbm, rows_ref),
                (counts_hbm, counts_ref),
                (features_hbm, features_ref),
                (dst_hbm, dst_ref),
                (src_hbm, src_ref),
            )
        )
    ]
    for move in moves:
        move.start()
    moves[0].wait()
    moves[1].wait()
    peers, capacity = rows_ref.shape[1:]
    slots = peers * capacity
    v_local = features_ref.shape[0]
    counts = counts_ref[...]
    to_peer = jnp.sum(
        jnp.where(iota((peers, peers), 1) == own_index(), counts, 0), axis=1, keepdims=True
    )
    from_peer = jnp.sum(
        jnp.where(iota((peers, peers), 0) == own_index(), counts, 0), axis=0, keepdims=True
    )
    live = iota((peers, capacity), 1) < to_peer
    index = jnp.where(live, rows_ref[0], -1)
    column = as_column(index.astype(jnp.float32).astype(jnp.bfloat16), slots)
    hot = ones(iota((slots, v_local), 1) == column)
    moves[2].wait()
    outgoing_ref[...] = rows_3d(dot32(hot, features_ref[...]), capacity)

    for move in moves[3:]:
        move.wait()
    tiles = dst_ref.shape[1]
    facts_ref[0:1, :tiles] = dst_ref[...]
    facts_ref[1:2, :tiles] = src_ref[...]
    facts_ref[8 : 8 + peers, :capacity] = index
    facts_ref[8 + peers : 9 + peers, :peers] = from_peer


def build_kernel(
    buffers,
    chunk,
    peers,
    used_ref,
    facts_hbm,
    masks_ref,
    adj_ref,
    counted_ref,
    index_row_ref,
    rest_ref,
    total,
    held,
    stage,
    tiles_ref,
    facts_ref,
    sems,
    stage_sem,
    small_sems,
):
    moves = [
        pltpu.make_async_copy(source, target, small_sems.at[at])
        for at, (source, target) in enumerate(
            ((facts_hbm.at[:8], tiles_ref), (facts_hbm.at[8:], facts_ref))
        )
    ]
    for move in moves:
        move.start()
    tile = masks_ref.shape[1]
    slots = adj_ref.shape[0]
    blocks = slots // tile
    capacity = slots // peers

    def fetch(step):
        slot = lax.rem(step, buffers)
        return pltpu.make_async_copy(
            masks_ref.at[pl.ds(step * chunk, chunk)], held.at[slot], sems.at[slot]
        )

    for step in range(buffers):
        fetch(step).start()

    def clear(block, carry):
        total[block] = jnp.zeros((tile, tile), jnp.int32)
        return carry

    lax.fori_loop(0, blocks * blocks, clear, 0)
    for move in moves:
        move.wait()
    used = used_ref[0]
    chunks = (used + chunk - 1) // chunk

    def one_chunk(step, carry):
        slot = lax.rem(step, buffers)
        fetch(step).wait()
        first = step * chunk

        def one_tile(at, inner):
            where = tiles_ref[0, first + at] * blocks + tiles_ref[1, first + at]
            total[where] += held[slot, at]
            return inner

        full = first + chunk <= used

        @pl.when(full)
        def _():
            for at in range(chunk):
                one_tile(at, 0)

        @pl.when(jnp.logical_not(full))
        def _():
            lax.fori_loop(0, used - first, one_tile, 0)

        @pl.when(step + buffers < chunks)
        def _():
            fetch(step + buffers).start()

        return carry

    lax.fori_loop(0, chunks, one_chunk, 0)
    for step in range(buffers):

        @pl.when(step >= chunks)
        def _():
            fetch(step).wait()


    index = facts_ref[:peers, :capacity].astype(jnp.float32).astype(jnp.bfloat16)
    index_row_ref[...] = as_row(index, slots)
    live_count = facts_ref[peers : peers + 1, :peers].astype(jnp.float32)
    live_count = jnp.broadcast_to(live_count, (8, peers))
    place = iota((peers, slots), 1) // capacity == iota((peers, slots), 0)
    spread = dot32(
        live_count.astype(jnp.bfloat16), ones(place)
    )
    live_row = (iota((8, slots), 1) % capacity < spread.astype(jnp.int32)).astype(jnp.float32)

    def one_row(row, most):
        counted = jnp.zeros((tile, tile), jnp.float32)
        at_row = pl.multiple_of(row * tile, tile)
        for col in range(blocks):
            value = total[row * blocks + col]
            most = jnp.maximum(most, value)
            value = value.astype(jnp.float32)
            counted = counted + value * live_row[:1, col * tile : (col + 1) * tile]
            low = jnp.minimum(value, float(EXACT))
            adj_ref[pl.ds(at_row, tile), col * tile : (col + 1) * tile] = low.astype(jnp.bfloat16)
        counted_ref[pl.ds(row, 1), :] = jnp.sum(counted.T, axis=0, keepdims=True)
        return most

    most = lax.fori_loop(0, blocks, one_row, jnp.zeros((tile, tile), jnp.int32))
    over = jnp.max(most) > EXACT
    counted_ref[blocks:, :] = jnp.full((8, tile), over.astype(jnp.float32))

    @pl.when(over)
    def _():
        def rest_row(row, carry):
            for col in range(blocks):
                value = jnp.maximum(total[row * blocks + col] - EXACT, 0)
                stage[:, col * tile : (col + 1) * tile] = value.astype(jnp.float32).astype(
                    jnp.bfloat16
                )
            copy = pltpu.make_async_copy(
                stage, rest_ref.at[pl.ds(pl.multiple_of(row * tile, tile), tile)], stage_sem
            )
            copy.start()
            copy.wait()
            return carry

        lax.fori_loop(0, blocks, rest_row, 0)


def forward_kernel(
    adj_ref,
    counted_ref,
    mirrored_ref,
    rest_ref,
    out_hbm,
    out_ref,
    more,
    stage,
    stage_sem,
    sems,
):
    peers, capacity, width = mirrored_ref.shape
    slots = peers * capacity
    tile = stage.shape[0]
    columns = width // LANES
    source = rows_2d(mirrored_ref[...])
    counted = counted_ref[: slots // tile, :]
    over = jnp.max(counted_ref[slots // tile :, :]) > 0
    high = jnp.floor(counted * (1.0 / EXACT))
    low = counted - high * EXACT
    per_group = LANES // capacity
    at_extra = columns * capacity
    extra = out_ref.shape[1] - at_extra
    which = iota((extra, LANES), 0)
    for group in range(slots // LANES):
        both = jnp.where(
            which == 0,
            high[group : group + 1],
            jnp.where(which == 1, low[group : group + 1], 0.0),
        ).astype(jnp.bfloat16)
        out_ref[group * per_group : (group + 1) * per_group, at_extra:, :] = jnp.broadcast_to(
            both[None], (per_group, extra, LANES)
        )

    def multiply(add_rest):
        pieces = Pieces(out_ref, out_hbm, sems, capacity)
        for piece in range(pieces.count):
            sums = dot32(adj_ref[pieces.slots(piece), :], source)
            if add_rest:
                sums += more[pieces.slots(piece), :]
            for col in range(columns):
                out_ref[pieces.rows(piece), col * capacity : (col + 1) * capacity, :] = rows_3d(
                    sums[:, col * LANES : (col + 1) * LANES], capacity
                )
            pieces.start(piece)
        pieces.wait()

    @pl.when(jnp.logical_not(over))
    def _():
        multiply(False)

    @pl.when(over)
    def _():
        for row in range(slots // tile):
            rows = slice(row * tile, (row + 1) * tile)
            copy = pltpu.make_async_copy(rest_ref.at[rows], stage, stage_sem)
            copy.start()
            copy.wait()
            more[rows, :] = dot32(stage[...], source)
        multiply(True)


def middle_kernel(
    index_ref,
    arrived_ref,
    features_ref,
    cotangent_ref,
    weight_self_ref,
    weight_neigh_ref,
    bias_ref,
    output_hbm,
    mean_hbm,
    grad_pre_hbm,
    out_hbm,
    output_ref,
    mean_ref,
    grad_pre_ref,
    stage,
    result_sems,
    out_sems,
):
    v_local, width = features_ref.shape
    peers = arrived_ref.shape[0]
    slots = index_ref.shape[1]
    capacity = slots // peers
    columns = width // LANES
    where = iota((v_local, slots), 0) == index_ref[...]
    hot = where.astype(jnp.float32).astype(jnp.bfloat16)

    extra = arrived_ref[:, columns * capacity :, :].astype(jnp.float32)
    both = jnp.concatenate([extra[:, 0, :], extra[:, 1, :]], axis=0).astype(jnp.bfloat16)
    section = lax.rem(own_index(), LANES // capacity) * capacity
    place = iota((LANES, slots), 0) == section + iota((LANES, slots), 1) % capacity
    spread = dot32(both, ones(place))
    counted = diagonal_row(spread[:peers] * float(EXACT) + spread[peers:], capacity)
    degrees = jnp.sum(jnp.where(where, counted, 0.0), axis=1, keepdims=True)
    divisor = jnp.maximum(degrees, 1.0)

    partial = jnp.concatenate(
        [
            rows_2d(arrived_ref[:, col * capacity : (col + 1) * capacity, :])
            for col in range(columns)
        ],
        axis=1,
    )
    mean_rows = (dot32(hot, partial) / divisor).astype(jnp.bfloat16)
    mean_ref[...] = mean_rows
    pre_act = (
        dot32(features_ref[...], weight_self_ref[...])
        + dot32(mean_rows, weight_neigh_ref[...])
        + bias_ref[...].astype(jnp.float32)
    )
    sigmoid_pre = 1.0 / (1.0 + jnp.exp(-pre_act))
    grad_pre32 = (
        cotangent_ref[...].astype(jnp.float32)
        * sigmoid_pre
        * (1.0 + pre_act * (1.0 - sigmoid_pre))
    )
    grad_pre = grad_pre32.astype(jnp.bfloat16)
    grad_mean = (dot_general32(grad_pre, weight_neigh_ref[...], NT) / divisor).astype(jnp.bfloat16)
    pieces = Pieces(stage, out_hbm, out_sems, capacity)
    for piece in range(pieces.count):
        picked = dot_general32(hot[:, pieces.slots(piece)], grad_mean, TN)
        pieces.send(piece, rows_3d(picked, capacity))
    grad_pre_ref[...] = grad_pre
    output_ref[...] = (pre_act * sigmoid_pre).astype(jnp.bfloat16)
    results = [
        pltpu.make_async_copy(source, target, result_sems.at[at])
        for at, (source, target) in enumerate(
            ((mean_ref, mean_hbm), (grad_pre_ref, grad_pre_hbm), (output_ref, output_hbm))
        )
    ]
    for result in results:
        result.start()
    pieces.wait()
    for result in results:
        result.wait()


def parts_kernel(features_ref, mean_ref, grad_pre_ref, keep_ref, send_ref):
    grad_pre = grad_pre_ref[...]
    width, d_out = features_ref.shape[1], grad_pre.shape[1]
    rows = keep_ref.shape[0]
    block = 2 * rows // GROUP
    for kind, rows_ref in enumerate((features_ref, mean_ref)):
        part = dot_general32(rows_ref[...], grad_pre, TN)
        for col in range(d_out // LANES):
            for step in range(width // block):
                number = (col * 2 + kind) * (width // block) + step
                place = number ^ own_group()
                value = part[step * block : (step + 1) * block, col * LANES : (col + 1) * LANES]

                @pl.when(place < GROUP // 2)
                def _():
                    keep_ref[pl.ds(pl.multiple_of(place * block, block), block), :] = value

                @pl.when(place >= GROUP // 2)
                def _():
                    at = pl.multiple_of((place - GROUP // 2) * block, block)
                    send_ref[pl.ds(at, block), :] = value

    part_bias = jnp.sum(grad_pre.astype(jnp.float32), axis=0, keepdims=True)
    which = iota((8, LANES), 0)
    bias_block = jnp.zeros((8, LANES), jnp.float32)
    for col in range(d_out // LANES):
        bias_block = jnp.where(
            which == col, part_bias[:, col * LANES : (col + 1) * LANES], bias_block
        )
    send_ref[rows:, :] = bias_block


def quarter_kernel(keep_ref, sent_ref, got_ref, own_ref, *other_refs):
    rows = keep_ref.shape[0]
    block = rows // 4
    for at, ref in enumerate((own_ref, *other_refs)):
        cut = slice(at * block, (at + 1) * block)
        ref[:block, :] = (keep_ref[cut, :] + got_ref[cut, :]).astype(ref.dtype)
        ref[block:, :] = (sent_ref[rows:, :] + got_ref[rows:, :]).astype(ref.dtype)


def backward_kernel(
    adj_ref, counted_ref, arrived_ref, rest_ref, out_hbm, out_ref, more, stage, stage_sem, sems
):
    peers, capacity, width = arrived_ref.shape
    tile = stage.shape[0]
    slots = peers * capacity
    source = rows_2d(arrived_ref[...])
    over = jnp.max(counted_ref[slots // tile :, :]) > 0
    source_t = source.astype(jnp.float32).T.astype(jnp.bfloat16)

    def multiply(add_rest):
        pieces = Pieces(out_ref, out_hbm, sems, capacity)
        for piece in range(pieces.count):
            sums = dot32(source_t, adj_ref[:, pieces.slots(piece)]).T
            if add_rest:
                sums += more[pieces.slots(piece), :]
            pieces.send(piece, rows_3d(sums, capacity))
        pieces.wait()

    @pl.when(jnp.logical_not(over))
    def _():
        multiply(False)

    @pl.when(over)
    def _():
        more[...] = jnp.zeros_like(more)
        for row in range(slots // tile):
            rows = slice(row * tile, (row + 1) * tile)
            copy = pltpu.make_async_copy(rest_ref.at[rows], stage, stage_sem)
            copy.start()
            copy.wait()
            more[...] += dot_general32(stage[...], source[rows], TN)
        multiply(True)


def layout_kernel(
    norm_scale,
    own_ref,
    near_1_ref,
    near_2_ref,
    near_3_ref,
    far_ref,
    self_ref,
    neigh_ref,
    bias_ref,
):
    block = near_1_ref.shape[0]
    near_refs = (near_1_ref, near_2_ref, near_3_ref)
    width, d_out = self_ref.shape
    per_part = width // block
    for place in range(GROUP):
        if place < 1:
            value = own_ref[:block, :]
        elif place < 4:
            value = near_refs[place - 1][...]
        else:
            value = far_ref[(place - 4) * block : (place - 3) * block, :]
        value = value.astype(jnp.float32) * norm_scale
        number = place ^ own_group()
        at = pl.multiple_of(lax.rem(number, per_part) * block, block)
        quarter = number // per_part
        for col in range(d_out // LANES):
            for kind, ref in enumerate((self_ref, neigh_ref)):

                @pl.when(quarter == col * 2 + kind)
                def _():
                    ref[pl.ds(at, block), col * LANES : (col + 1) * LANES] = value

    for col in range(d_out // LANES):
        bias_ref[:, col * LANES : (col + 1) * LANES] = (
            own_ref[block + col : block + col + 1, :].astype(jnp.float32) * norm_scale
        )


def end_kernel(index_ref, arrived_ref, grad_pre_ref, weight_self_ref, grad_x_ref):
    v_local = grad_x_ref.shape[0]
    hot = one_hot(index_ref[...], v_local)
    own = dot_general32(grad_pre_ref[...], weight_self_ref[...], NT)
    back = dot32(hot, rows_2d(arrived_ref[...]))
    grad_x_ref[...] = (own + back).astype(jnp.bfloat16)


def in_smem():
    return pl.BlockSpec(memory_space=pltpu.SMEM)


def in_vmem():
    return pl.BlockSpec(memory_space=pltpu.VMEM)


def in_hbm():
    return pl.BlockSpec(memory_space=pltpu.HBM)


def exchange(block):
    return lax.all_to_all(block, AXES, split_axis=0, concat_axis=0, tiled=True)


def swap(block, axis, bit):
    size = lax.axis_size(axis)
    return lax.ppermute(block, axis, [(at, at ^ bit) for at in range(size)])


def per_device(
    features,
    cotangent,
    weight_self,
    weight_neigh,
    layer_bias,
    mirror_rows,
    mirror_counts,
    tile_count,
    tile_rows,
    tile_cols,
    tile_masks,
):
    f32, bf16, i32 = jnp.float32, jnp.bfloat16, jnp.int32
    v_local, width = features.shape
    d_out = weight_self.shape[1]
    peers, capacity = mirror_rows.shape[1:]
    slots = peers * capacity
    masks = tile_masks[0]
    tiles_max, tile = masks.shape[:2]
    blocks = slots // tile
    pieces = width // LANES
    rows = 2 * width * (d_out // LANES)
    shape = jax.ShapeDtypeStruct

    facts_shape = (8 + peers + 8, -(-tiles_max // LANES) * LANES)
    facts, outgoing = pl.pallas_call(
        gather_kernel,
        out_shape=(shape(facts_shape, i32), shape((peers, capacity, width), bf16)),
        in_specs=[in_hbm()] * 5,
        out_specs=(in_vmem(), in_vmem()),
        scratch_shapes=[
            pltpu.VMEM(mirror_rows.shape, i32),
            pltpu.VMEM(mirror_counts.shape, i32),
            pltpu.VMEM(features.shape, bf16),
            pltpu.VMEM(tile_rows.shape, i32),
            pltpu.VMEM(tile_cols.shape, i32),
            pltpu.SemaphoreType.DMA((5,)),
        ],
        compiler_params=pltpu.CompilerParams(vmem_limit_bytes=60 * MIB),
        name="gather_rows",
    )(mirror_rows, mirror_counts, features, tile_rows, tile_cols)

    mirrored = exchange(outgoing)

    chunk = math.gcd(8, tiles_max)
    buffers = min(8, tiles_max // chunk)
    adj, counted, index_row, rest = pl.pallas_call(
        functools.partial(build_kernel, buffers, chunk, peers),
        out_shape=(
            shape((slots, slots), bf16),
            shape((blocks + 8, tile), f32),
            shape((1, slots), i32),
            shape((REST_ROOM * slots, slots), bf16),
        ),
        in_specs=[in_smem()] + [in_hbm()] * 2,
        out_specs=(in_vmem(),) * 3 + (in_hbm(),),
        scratch_shapes=[
            pltpu.VMEM((blocks * blocks, tile, tile), i32),
            pltpu.VMEM((buffers, chunk, tile, tile), i32),
            pltpu.VMEM((tile, slots), bf16),
            pltpu.SMEM((8, facts_shape[1]), i32),
            pltpu.VMEM((facts_shape[0] - 8, facts_shape[1]), i32),
            pltpu.SemaphoreType.DMA((buffers,)),
            pltpu.SemaphoreType.DMA,
            pltpu.SemaphoreType.DMA((2,)),
        ],
        compiler_params=pltpu.CompilerParams(vmem_limit_bytes=48 * MIB),
        cost_estimate=pl.CostEstimate(
            flops=4 * tiles_max * tile * tile,
            bytes_accessed=masks.size * 4,
            transcendentals=0,
        ),
        name="build_counts",
    )(tile_count, facts, masks)

    partial_shape = (peers, pieces * capacity + 8, LANES)
    partial = pl.pallas_call(
        forward_kernel,
        out_shape=shape(partial_shape, bf16),
        in_specs=[in_vmem(), in_vmem(), in_vmem(), in_hbm()],
        out_specs=in_hbm(),
        scratch_shapes=[
            pltpu.VMEM(partial_shape, bf16),
            pltpu.VMEM((slots, width), f32),
            pltpu.VMEM((tile, slots), bf16),
            pltpu.SemaphoreType.DMA,
            pltpu.SemaphoreType.DMA((PIECES,)),
        ],
        compiler_params=pltpu.CompilerParams(vmem_limit_bytes=8 * MIB),
        name="forward_sums",
    )(adj, counted, mirrored, rest)

    arrived = exchange(partial)

    output, mean_rows, grad_pre, sent_back = pl.pallas_call(
        middle_kernel,
        out_shape=(
            shape((v_local, d_out), bf16),
            shape((v_local, width), bf16),
            shape((v_local, d_out), bf16),
            shape((peers, capacity, width), bf16),
        ),
        in_specs=[in_vmem()] * 7,
        out_specs=(in_hbm(),) * 4,
        scratch_shapes=[
            pltpu.VMEM((v_local, d_out), bf16),
            pltpu.VMEM((v_local, width), bf16),
            pltpu.VMEM((v_local, d_out), bf16),
            pltpu.VMEM((peers, capacity, width), bf16),
            pltpu.SemaphoreType.DMA((3,)),
            pltpu.SemaphoreType.DMA((PIECES,)),
        ],
        compiler_params=pltpu.CompilerParams(vmem_limit_bytes=6 * MIB),
        name="vertex_update",
    )(
        index_row,
        arrived,
        features,
        cotangent,
        weight_self,
        weight_neigh,
        layer_bias.reshape(1, d_out),
    )

    mirrored_grads = exchange(sent_back)

    keep, send = pl.pallas_call(
        parts_kernel,
        out_shape=(
            shape((rows // 2, LANES), f32),
            shape((rows // 2 + 8, LANES), f32),
        ),
        in_specs=[in_vmem()] * 3,
        out_specs=(in_vmem(),) * 2,
        compiler_params=pltpu.CompilerParams(vmem_limit_bytes=24 * MIB),
        cost_estimate=pl.CostEstimate(flops=1 << 27, bytes_accessed=1 << 20, transcendentals=0),
        name="weight_parts",
    )(features, mean_rows, grad_pre)

    got = swap(send, "dom", 1)
    own, *others = pl.pallas_call(
        quarter_kernel,
        out_shape=tuple(shape((rows // GROUP + 8, LANES), kind) for kind in (f32, bf16, bf16, bf16)),
        in_specs=[in_vmem()] * 3,
        out_specs=(in_vmem(),) * 4,
        compiler_params=pltpu.CompilerParams(vmem_limit_bytes=2 * MIB),
        name="quarter_sums",
    )(keep, send, got)
    got = [swap(other, "grp", bit) for bit, other in zip((1, 2, 3), others, strict=True)]
    full = (own + got[0].astype(f32)) + (got[1].astype(f32) + got[2].astype(f32))
    bit = 2
    while bit < lax.axis_size("dom"):
        sent = full.astype(bf16)
        got = [
            swap(sent, "dom", other)
            for other in (bit, 2 * bit, 3 * bit)
            if other < lax.axis_size("dom")
        ]
        wide = [value.astype(f32) for value in (sent, *got)]
        full = wide[0] + wide[1]
        if len(wide) == 4:
            full = full + (wide[2] + wide[3])
        bit *= 4
    full, mirrored_grads = lax.optimization_barrier((full, mirrored_grads))
    back_partial = pl.pallas_call(
        backward_kernel,
        out_shape=shape((peers, capacity, width), bf16),
        in_specs=[in_vmem(), in_vmem(), in_vmem(), in_hbm()],
        out_specs=in_hbm(),
        scratch_shapes=[
            pltpu.VMEM((peers, capacity, width), bf16),
            pltpu.VMEM((slots, width), f32),
            pltpu.VMEM((tile, slots), bf16),
            pltpu.SemaphoreType.DMA,
            pltpu.SemaphoreType.DMA((PIECES,)),
        ],
        compiler_params=pltpu.CompilerParams(vmem_limit_bytes=32 * MIB),
        cost_estimate=pl.CostEstimate(flops=1 << 29, bytes_accessed=3 << 20, transcendentals=0),
        name="backward_sums",
    )(adj, counted, mirrored_grads, rest)

    back_arrived = exchange(back_partial)

    full = full.astype(bf16)
    block = full[: rows // GROUP]
    near = [swap(block, "grp", bit) for bit in (1, 2, 3)]
    far = swap(jnp.concatenate([block, *near]), "dom", 1)

    norm_scale = 1.0 / math.sqrt(v_local * peers)
    grad_self, grad_neigh, grad_bias = pl.pallas_call(
        functools.partial(layout_kernel, norm_scale),
        out_shape=(
            shape((width, d_out), f32),
            shape((width, d_out), f32),
            shape((1, d_out), f32),
        ),
        in_specs=[in_vmem()] * 5,
        out_specs=(in_vmem(),) * 3,
        compiler_params=pltpu.CompilerParams(vmem_limit_bytes=8 * MIB),
        name="weight_layout",
    )(full, *near, far)

    grad_x = pl.pallas_call(
        end_kernel,
        out_shape=shape((v_local, width), bf16),
        in_specs=[in_vmem()] * 4,
        out_specs=in_vmem(),
        compiler_params=pltpu.CompilerParams(vmem_limit_bytes=24 * MIB),
        name="vertex_grads",
    )(index_row, back_arrived, grad_pre, weight_self)

    return output, grad_x, grad_self, grad_neigh, grad_bias.reshape(d_out)


def solution(mesh):
    in_specs = (
        P(AXES, None),
        P(AXES, None),
        P(),
        P(),
        P(),
        P(AXES, None, None),
        P(),
        P(AXES),
        P(AXES, None),
        P(AXES, None),
        P(AXES, None, None, None),
    )
    out_specs = (P(AXES, None), P(AXES, None), P(), P(), P())
    return jax.shard_map(
        per_device, mesh=mesh, in_specs=in_specs, out_specs=out_specs, check_vma=False
    )
```

```python
import functools
import math

import jax
import jax.numpy as jnp
from jax import lax
from jax.experimental import pallas as pl
from jax.experimental.pallas import tpu as pltpu
from jax.sharding import PartitionSpec as P

AXES = ("grp", "dom")
LANES = 128
EXACT = 256
MIB = 1 << 20
PIECES = 4
REST_ROOM = 24
GROUP = 8

NT = (((1,), (1,)), ((), ()))
TN = (((0,), (0,)), ((), ()))


def own_index():
    return lax.axis_index(AXES)


def own_group():
    return (lax.axis_index("dom") & 1) * 4 + (lax.axis_index("grp") & 3)


def dot32(a, b):
    return jnp.dot(a, b, preferred_element_type=jnp.float32)


def dot_general32(a, b, dims):
    return lax.dot_general(a, b, dims, preferred_element_type=jnp.float32)


def iota(shape, dim):
    return lax.broadcasted_iota(jnp.int32, shape, dim)


def rows_2d(block):
    peers, rows, width = block.shape
    if rows % 16 == 0:
        return block.reshape(peers * rows, width)
    return block.astype(jnp.float32).reshape(peers * rows, width).astype(block.dtype)


def rows_3d(block, rows):
    return block.reshape(block.shape[0] // rows, rows, block.shape[1]).astype(jnp.bfloat16)


class Pieces:
    def __init__(self, out, capacity):
        self.count = PIECES
        self.peers = out.shape[0] // PIECES
        self.capacity = capacity

    def rows(self, piece):
        return slice(piece * self.peers, (piece + 1) * self.peers)

    def slots(self, piece):
        per_piece = self.peers * self.capacity
        return slice(piece * per_piece, (piece + 1) * per_piece)


def diagonal_row(spread, capacity):
    peers, slots = spread.shape
    own = iota((peers, slots), 1) // capacity == iota((peers, slots), 0)
    return jnp.sum(jnp.where(own, spread, 0.0), axis=0, keepdims=True)


def ones(mask):
    return mask.astype(jnp.float32).astype(jnp.bfloat16)


def one_hot(index_row, v_local):
    return ones(iota((v_local, index_row.shape[1]), 0) == index_row)


def as_column(index, slots):
    peers, capacity = index.shape
    spread = dot32(ones(iota((slots, peers), 0) // capacity == iota((slots, peers), 1)), index)
    own = iota((slots, capacity), 0) % capacity == iota((slots, capacity), 1)
    return jnp.sum(jnp.where(own, spread, 0.0), axis=1, keepdims=True).astype(jnp.int32)


def as_row(index, slots):
    capacity = index.shape[1]
    place = ones(iota((capacity, slots), 1) % capacity == iota((capacity, slots), 0))
    return diagonal_row(dot32(index, place), capacity).astype(jnp.int32)


def gather_kernel(
    rows_hbm,
    counts_hbm,
    features_hbm,
    dst_hbm,
    src_hbm,
    facts_ref,
    outgoing_ref,
    rows_ref,
    counts_ref,
    features_ref,
    dst_ref,
    src_ref,
    sems,
):
    moves = [
        pltpu.make_async_copy(source, target, sems.at[at])
        for at, (source, target) in enumerate(
            (
                (rows_hbm, rows_ref),
                (counts_hbm, counts_ref),
                (features_hbm, features_ref),
                (dst_hbm, dst_ref),
                (src_hbm, src_ref),
            )
        )
    ]
    for move in moves:
        move.start()
    moves[0].wait()
    moves[1].wait()
    peers, capacity = rows_ref.shape[1:]
    slots = peers * capacity
    v_local = features_ref.shape[0]
    counts = counts_ref[...]
    to_peer = jnp.sum(
        jnp.where(iota((peers, peers), 1) == own_index(), counts, 0), axis=1, keepdims=True
    )
    from_peer = jnp.sum(
        jnp.where(iota((peers, peers), 0) == own_index(), counts, 0), axis=0, keepdims=True
    )
    live = iota((peers, capacity), 1) < to_peer
    index = jnp.where(live, rows_ref[0], -1)
    column = as_column(index.astype(jnp.float32).astype(jnp.bfloat16), slots)
    hot = ones(iota((slots, v_local), 1) == column)
    moves[2].wait()
    outgoing_ref[...] = rows_3d(dot32(hot, features_ref[...]), capacity)

    for move in moves[3:]:
        move.wait()
    tiles = dst_ref.shape[1]
    facts_ref[0:1, :tiles] = dst_ref[...]
    facts_ref[1:2, :tiles] = src_ref[...]
    facts_ref[8 : 8 + peers, :capacity] = index
    facts_ref[8 + peers : 9 + peers, :peers] = from_peer


def build_kernel(
    buffers,
    chunk,
    peers,
    used_ref,
    facts_hbm,
    masks_ref,
    adj_ref,
    counted_ref,
    index_row_ref,
    rest_ref,
    total,
    held,
    stage,
    tiles_ref,
    facts_ref,
    sems,
    stage_sem,
    small_sems,
):
    moves = [
        pltpu.make_async_copy(source, target, small_sems.at[at])
        for at, (source, target) in enumerate(
            ((facts_hbm.at[:8], tiles_ref), (facts_hbm.at[8:], facts_ref))
        )
    ]
    for move in moves:
        move.start()
    tile = masks_ref.shape[1]
    slots = adj_ref.shape[0]
    blocks = slots // tile
    capacity = slots // peers

    def fetch(step):
        slot = lax.rem(step, buffers)
        return pltpu.make_async_copy(
            masks_ref.at[pl.ds(step * chunk, chunk)], held.at[slot], sems.at[slot]
        )

    for step in range(buffers):
        fetch(step).start()

    def clear(block, carry):
        total[block] = jnp.zeros((tile, tile), jnp.int32)
        return carry

    lax.fori_loop(0, blocks * blocks, clear, 0)
    for move in moves:
        move.wait()
    used = used_ref[0]
    chunks = (used + chunk - 1) // chunk

    def one_chunk(step, carry):
        slot = lax.rem(step, buffers)
        fetch(step).wait()
        first = step * chunk

        def one_tile(at, inner):
            where = tiles_ref[0, first + at] * blocks + tiles_ref[1, first + at]
            total[where] += held[slot, at]
            return inner

        full = first + chunk <= used

        @pl.when(full)
        def _():
            for at in range(chunk):
                one_tile(at, 0)

        @pl.when(jnp.logical_not(full))
        def _():
            lax.fori_loop(0, used - first, one_tile, 0)

        @pl.when(step + buffers < chunks)
        def _():
            fetch(step + buffers).start()

        return carry

    lax.fori_loop(0, chunks, one_chunk, 0)
    for step in range(buffers):

        @pl.when(step >= chunks)
        def _():
            fetch(step).wait()


    index = facts_ref[:peers, :capacity].astype(jnp.float32).astype(jnp.bfloat16)
    index_row_ref[...] = as_row(index, slots)
    live_count = facts_ref[peers : peers + 1, :peers].astype(jnp.float32)
    live_count = jnp.broadcast_to(live_count, (8, peers))
    place = iota((peers, slots), 1) // capacity == iota((peers, slots), 0)
    spread = dot32(
        live_count.astype(jnp.bfloat16), ones(place)
    )
    live_row = (iota((8, slots), 1) % capacity < spread.astype(jnp.int32)).astype(jnp.float32)

    def one_row(row, most):
        counted = jnp.zeros((tile, tile), jnp.float32)
        at_row = pl.multiple_of(row * tile, tile)
        for col in range(blocks):
            value = total[row * blocks + col]
            most = jnp.maximum(most, value)
            value = value.astype(jnp.float32)
            counted = counted + value * live_row[:1, col * tile : (col + 1) * tile]
            low = jnp.minimum(value, float(EXACT))
            adj_ref[pl.ds(at_row, tile), col * tile : (col + 1) * tile] = low.astype(jnp.bfloat16)
        counted_ref[pl.ds(row, 1), :] = jnp.sum(counted.T, axis=0, keepdims=True)
        return most

    most = lax.fori_loop(0, blocks, one_row, jnp.zeros((tile, tile), jnp.int32))
    over = jnp.max(most) > EXACT
    counted_ref[blocks:, :] = jnp.full((8, tile), over.astype(jnp.float32))

    @pl.when(over)
    def _():
        def rest_row(row, carry):
            for col in range(blocks):
                value = jnp.maximum(total[row * blocks + col] - EXACT, 0)
                stage[:, col * tile : (col + 1) * tile] = value.astype(jnp.float32).astype(
                    jnp.bfloat16
                )
            copy = pltpu.make_async_copy(
                stage, rest_ref.at[pl.ds(pl.multiple_of(row * tile, tile), tile)], stage_sem
            )
            copy.start()
            copy.wait()
            return carry

        lax.fori_loop(0, blocks, rest_row, 0)


def forward_kernel(
    adj_ref,
    counted_ref,
    mirrored_ref,
    rest_ref,
    out_ref,
    more,
    stage,
    stage_sem,
):
    peers, capacity, width = mirrored_ref.shape
    slots = peers * capacity
    tile = stage.shape[0]
    columns = width // LANES
    source = rows_2d(mirrored_ref[...])
    counted = counted_ref[: slots // tile, :]
    over = jnp.max(counted_ref[slots // tile :, :]) > 0
    high = jnp.floor(counted * (1.0 / EXACT))
    low = counted - high * EXACT
    per_group = LANES // capacity
    at_extra = columns * capacity
    extra = out_ref.shape[1] - at_extra
    which = iota((extra, LANES), 0)
    for group in range(slots // LANES):
        both = jnp.where(
            which == 0,
            high[group : group + 1],
            jnp.where(which == 1, low[group : group + 1], 0.0),
        ).astype(jnp.bfloat16)
        out_ref[group * per_group : (group + 1) * per_group, at_extra:, :] = jnp.broadcast_to(
            both[None], (per_group, extra, LANES)
        )

    def multiply(add_rest):
        pieces = Pieces(out_ref, capacity)
        for piece in range(pieces.count):
            sums = dot32(adj_ref[pieces.slots(piece), :], source)
            if add_rest:
                sums += more[pieces.slots(piece), :]
            for col in range(columns):
                out_ref[pieces.rows(piece), col * capacity : (col + 1) * capacity, :] = rows_3d(
                    sums[:, col * LANES : (col + 1) * LANES], capacity
                )

    @pl.when(jnp.logical_not(over))
    def _():
        multiply(False)

    @pl.when(over)
    def _():
        for row in range(slots // tile):
            rows = slice(row * tile, (row + 1) * tile)
            copy = pltpu.make_async_copy(rest_ref.at[rows], stage, stage_sem)
            copy.start()
            copy.wait()
            more[rows, :] = dot32(stage[...], source)
        multiply(True)


def middle_kernel(
    index_ref,
    arrived_ref,
    features_ref,
    cotangent_ref,
    weight_self_ref,
    weight_neigh_ref,
    bias_ref,
    output_ref,
    mean_ref,
    grad_pre_ref,
    out_ref,
):
    v_local, width = features_ref.shape
    peers = arrived_ref.shape[0]
    slots = index_ref.shape[1]
    capacity = slots // peers
    columns = width // LANES
    where = iota((v_local, slots), 0) == index_ref[...]
    hot = where.astype(jnp.float32).astype(jnp.bfloat16)

    extra = arrived_ref[:, columns * capacity :, :].astype(jnp.float32)
    both = jnp.concatenate([extra[:, 0, :], extra[:, 1, :]], axis=0).astype(jnp.bfloat16)
    section = lax.rem(own_index(), LANES // capacity) * capacity
    place = iota((LANES, slots), 0) == section + iota((LANES, slots), 1) % capacity
    spread = dot32(both, ones(place))
    counted = diagonal_row(spread[:peers] * float(EXACT) + spread[peers:], capacity)
    degrees = jnp.sum(jnp.where(where, counted, 0.0), axis=1, keepdims=True)
    divisor = jnp.maximum(degrees, 1.0)

    partial = jnp.concatenate(
        [
            rows_2d(arrived_ref[:, col * capacity : (col + 1) * capacity, :])
            for col in range(columns)
        ],
        axis=1,
    )
    mean_rows = (dot32(hot, partial) / divisor).astype(jnp.bfloat16)
    mean_ref[...] = mean_rows
    pre_act = (
        dot32(features_ref[...], weight_self_ref[...])
        + dot32(mean_rows, weight_neigh_ref[...])
        + bias_ref[...].astype(jnp.float32)
    )
    sigmoid_pre = 1.0 / (1.0 + jnp.exp(-pre_act))
    grad_pre32 = (
        cotangent_ref[...].astype(jnp.float32)
        * sigmoid_pre
        * (1.0 + pre_act * (1.0 - sigmoid_pre))
    )
    grad_pre = grad_pre32.astype(jnp.bfloat16)
    grad_mean = (dot_general32(grad_pre, weight_neigh_ref[...], NT) / divisor).astype(jnp.bfloat16)
    grad_pre_ref[...] = grad_pre
    output_ref[...] = (pre_act * sigmoid_pre).astype(jnp.bfloat16)
    out_ref[...] = rows_3d(dot_general32(hot, grad_mean, TN), capacity)


def parts_kernel(features_ref, mean_ref, grad_pre_ref, keep_ref, send_ref):
    grad_pre = grad_pre_ref[...]
    width, d_out = features_ref.shape[1], grad_pre.shape[1]
    rows = keep_ref.shape[0]
    block = 2 * rows // GROUP
    for kind, rows_ref in enumerate((features_ref, mean_ref)):
        part = dot_general32(rows_ref[...], grad_pre, TN)
        for col in range(d_out // LANES):
            for step in range(width // block):
                number = (col * 2 + kind) * (width // block) + step
                place = number ^ own_group()
                value = part[step * block : (step + 1) * block, col * LANES : (col + 1) * LANES]

                @pl.when(place < GROUP // 2)
                def _():
                    keep_ref[pl.ds(pl.multiple_of(place * block, block), block), :] = value

                @pl.when(place >= GROUP // 2)
                def _():
                    at = pl.multiple_of((place - GROUP // 2) * block, block)
                    send_ref[pl.ds(at, block), :] = value

    part_bias = jnp.sum(grad_pre.astype(jnp.float32), axis=0, keepdims=True)
    which = iota((8, LANES), 0)
    bias_block = jnp.zeros((8, LANES), jnp.float32)
    for col in range(d_out // LANES):
        bias_block = jnp.where(
            which == col, part_bias[:, col * LANES : (col + 1) * LANES], bias_block
        )
    send_ref[rows:, :] = bias_block


def quarter_kernel(keep_ref, sent_ref, got_ref, own_ref, *other_refs):
    rows = keep_ref.shape[0]
    block = rows // 4
    bias = (sent_ref[rows:, :] + got_ref[rows:, :]).astype(jnp.bfloat16)
    for at, ref in enumerate((own_ref, *other_refs)):
        cut = slice(at * block, (at + 1) * block)
        ref[:block, :] = (keep_ref[cut, :] + got_ref[cut, :]).astype(ref.dtype)
        ref[block:, :] = bias.astype(ref.dtype)


def backward_kernel(
    adj_ref, counted_ref, arrived_ref, rest_ref, out_ref, more, stage, stage_sem
):
    peers, capacity, width = arrived_ref.shape
    tile = stage.shape[0]
    slots = peers * capacity
    source = rows_2d(arrived_ref[...])
    over = jnp.max(counted_ref[slots // tile :, :]) > 0
    source_t = source.astype(jnp.float32).T.astype(jnp.bfloat16)

    def multiply(add_rest):
        pieces = Pieces(out_ref, capacity)
        for piece in range(pieces.count):
            sums = dot32(source_t, adj_ref[:, pieces.slots(piece)]).T
            if add_rest:
                sums += more[pieces.slots(piece), :]
            out_ref[pieces.rows(piece)] = rows_3d(sums, capacity)

    @pl.when(jnp.logical_not(over))
    def _():
        multiply(False)

    @pl.when(over)
    def _():
        more[...] = jnp.zeros_like(more)
        for row in range(slots // tile):
            rows = slice(row * tile, (row + 1) * tile)
            copy = pltpu.make_async_copy(rest_ref.at[rows], stage, stage_sem)
            copy.start()
            copy.wait()
            more[...] += dot_general32(stage[...], source[rows], TN)
        multiply(True)


def layout_kernel(
    norm_scale,
    own_ref,
    near_1_ref,
    near_2_ref,
    near_3_ref,
    far_ref,
    self_ref,
    neigh_ref,
    bias_ref,
):
    block = near_1_ref.shape[0]
    near_refs = (near_1_ref, near_2_ref, near_3_ref)
    width, d_out = self_ref.shape
    per_part = width // block
    for place in range(GROUP):
        if place < 1:
            value = own_ref[:block, :]
        elif place < 4:
            value = near_refs[place - 1][...]
        else:
            value = far_ref[(place - 4) * block : (place - 3) * block, :]
        value = value.astype(jnp.float32) * norm_scale
        number = place ^ own_group()
        at = pl.multiple_of(lax.rem(number, per_part) * block, block)
        quarter = number // per_part
        for col in range(d_out // LANES):
            for kind, ref in enumerate((self_ref, neigh_ref)):

                @pl.when(quarter == col * 2 + kind)
                def _():
                    ref[pl.ds(at, block), col * LANES : (col + 1) * LANES] = value

    for col in range(d_out // LANES):
        bias_ref[:, col * LANES : (col + 1) * LANES] = (
            own_ref[block + col : block + col + 1, :].astype(jnp.float32) * norm_scale
        )


def end_kernel(index_ref, arrived_ref, grad_pre_ref, weight_self_ref, grad_x_ref):
    v_local = grad_x_ref.shape[0]
    hot = one_hot(index_ref[...], v_local)
    own = dot_general32(grad_pre_ref[...], weight_self_ref[...], NT)
    back = dot32(hot, rows_2d(arrived_ref[...]))
    grad_x_ref[...] = (own + back).astype(jnp.bfloat16)


def in_smem():
    return pl.BlockSpec(memory_space=pltpu.SMEM)


def in_vmem():
    return pl.BlockSpec(memory_space=pltpu.VMEM)


def in_hbm():
    return pl.BlockSpec(memory_space=pltpu.HBM)


def exchange(block):
    return lax.all_to_all(block, AXES, split_axis=0, concat_axis=0, tiled=True)


def swap(block, axis, bit):
    size = lax.axis_size(axis)
    return lax.ppermute(block, axis, [(at, at ^ bit) for at in range(size)])


def per_device(
    features,
    cotangent,
    weight_self,
    weight_neigh,
    layer_bias,
    mirror_rows,
    mirror_counts,
    tile_count,
    tile_rows,
    tile_cols,
    tile_masks,
):
    f32, bf16, i32 = jnp.float32, jnp.bfloat16, jnp.int32
    v_local, width = features.shape
    d_out = weight_self.shape[1]
    peers, capacity = mirror_rows.shape[1:]
    slots = peers * capacity
    masks = tile_masks[0]
    tiles_max, tile = masks.shape[:2]
    blocks = slots // tile
    pieces = width // LANES
    rows = 2 * width * (d_out // LANES)
    shape = jax.ShapeDtypeStruct

    facts_shape = (8 + peers + 8, -(-tiles_max // LANES) * LANES)
    facts, outgoing = pl.pallas_call(
        gather_kernel,
        out_shape=(shape(facts_shape, i32), shape((peers, capacity, width), bf16)),
        in_specs=[in_hbm()] * 5,
        out_specs=(in_vmem(), in_vmem()),
        scratch_shapes=[
            pltpu.VMEM(mirror_rows.shape, i32),
            pltpu.VMEM(mirror_counts.shape, i32),
            pltpu.VMEM(features.shape, bf16),
            pltpu.VMEM(tile_rows.shape, i32),
            pltpu.VMEM(tile_cols.shape, i32),
            pltpu.SemaphoreType.DMA((5,)),
        ],
        compiler_params=pltpu.CompilerParams(vmem_limit_bytes=60 * MIB),
        name="gather_rows",
    )(mirror_rows, mirror_counts, features, tile_rows, tile_cols)

    mirrored = exchange(outgoing)

    chunk = math.gcd(8, tiles_max)
    buffers = min(8, tiles_max // chunk)
    adj, counted, index_row, rest = pl.pallas_call(
        functools.partial(build_kernel, buffers, chunk, peers),
        out_shape=(
            shape((slots, slots), bf16),
            shape((blocks + 8, tile), f32),
            shape((1, slots), i32),
            shape((REST_ROOM * slots, slots), bf16),
        ),
        in_specs=[in_smem()] + [in_hbm()] * 2,
        out_specs=(in_vmem(),) * 3 + (in_hbm(),),
        scratch_shapes=[
            pltpu.VMEM((blocks * blocks, tile, tile), i32),
            pltpu.VMEM((buffers, chunk, tile, tile), i32),
            pltpu.VMEM((tile, slots), bf16),
            pltpu.SMEM((8, facts_shape[1]), i32),
            pltpu.VMEM((facts_shape[0] - 8, facts_shape[1]), i32),
            pltpu.SemaphoreType.DMA((buffers,)),
            pltpu.SemaphoreType.DMA,
            pltpu.SemaphoreType.DMA((2,)),
        ],
        compiler_params=pltpu.CompilerParams(vmem_limit_bytes=48 * MIB),
        cost_estimate=pl.CostEstimate(
            flops=4 * tiles_max * tile * tile,
            bytes_accessed=masks.size * 4,
            transcendentals=0,
        ),
        name="build_counts",
    )(tile_count, facts, masks)

    partial_shape = (peers, pieces * capacity + 8, LANES)
    partial = pl.pallas_call(
        forward_kernel,
        out_shape=shape(partial_shape, bf16),
        in_specs=[in_vmem(), in_vmem(), in_vmem(), in_hbm()],
        out_specs=in_vmem(),
        scratch_shapes=[
            pltpu.VMEM((slots, width), f32),
            pltpu.VMEM((tile, slots), bf16),
            pltpu.SemaphoreType.DMA,
        ],
        compiler_params=pltpu.CompilerParams(vmem_limit_bytes=40 * MIB),
        name="forward_sums",
    )(adj, counted, mirrored, rest)

    arrived = exchange(partial)

    output, mean_rows, grad_pre, sent_back = pl.pallas_call(
        middle_kernel,
        out_shape=(
            shape((v_local, d_out), bf16),
            shape((v_local, width), bf16),
            shape((v_local, d_out), bf16),
            shape((peers, capacity, width), bf16),
        ),
        in_specs=[in_vmem()] * 7,
        out_specs=(in_vmem(),) * 4,
        compiler_params=pltpu.CompilerParams(vmem_limit_bytes=12 * MIB),
        name="vertex_update",
    )(
        index_row,
        arrived,
        features,
        cotangent,
        weight_self,
        weight_neigh,
        layer_bias.reshape(1, d_out),
    )

    mirrored_grads = exchange(sent_back)

    keep, send = pl.pallas_call(
        parts_kernel,
        out_shape=(
            shape((rows // 2, LANES), f32),
            shape((rows // 2 + 8, LANES), f32),
        ),
        in_specs=[in_vmem()] * 3,
        out_specs=(in_vmem(),) * 2,
        compiler_params=pltpu.CompilerParams(vmem_limit_bytes=8 * MIB),
        cost_estimate=pl.CostEstimate(flops=1 << 27, bytes_accessed=1 << 20, transcendentals=0),
        name="weight_parts",
    )(features, mean_rows, grad_pre)

    got = swap(send, "dom", 1)
    own, *others = pl.pallas_call(
        quarter_kernel,
        out_shape=tuple(shape((rows // GROUP + 8, LANES), kind) for kind in (f32, bf16, bf16, bf16)),
        in_specs=[in_vmem()] * 3,
        out_specs=(in_vmem(),) * 4,
        compiler_params=pltpu.CompilerParams(vmem_limit_bytes=4 * MIB),
        name="quarter_sums",
    )(keep, send, got)
    got = [swap(other, "grp", bit) for bit, other in zip((1, 2, 3), others, strict=True)]
    full = (own + got[0].astype(f32)) + (got[1].astype(f32) + got[2].astype(f32))
    bit = 2
    while bit < lax.axis_size("dom"):
        sent = full.astype(bf16)
        got = [
            swap(sent, "dom", other)
            for other in (bit, 2 * bit, 3 * bit)
            if other < lax.axis_size("dom")
        ]
        wide = [value.astype(f32) for value in (sent, *got)]
        full = wide[0] + wide[1]
        if len(wide) == 4:
            full = full + (wide[2] + wide[3])
        bit *= 4
    full, mirrored_grads = lax.optimization_barrier((full, mirrored_grads))
    back_partial = pl.pallas_call(
        backward_kernel,
        out_shape=shape((peers, capacity, width), bf16),
        in_specs=[in_vmem(), in_vmem(), in_vmem(), in_hbm()],
        out_specs=in_vmem(),
        scratch_shapes=[
            pltpu.VMEM((slots, width), f32),
            pltpu.VMEM((tile, slots), bf16),
            pltpu.SemaphoreType.DMA,
        ],
        compiler_params=pltpu.CompilerParams(vmem_limit_bytes=8 * MIB),
        cost_estimate=pl.CostEstimate(flops=1 << 29, bytes_accessed=3 << 20, transcendentals=0),
        name="backward_sums",
    )(adj, counted, mirrored_grads, rest)

    back_arrived = exchange(back_partial)

    full = full.astype(bf16)
    block = full[: rows // GROUP]
    near = [swap(block, "grp", bit) for bit in (1, 2, 3)]
    far = swap(jnp.concatenate([block, *near]), "dom", 1)

    norm_scale = 1.0 / math.sqrt(v_local * peers)
    grad_self, grad_neigh, grad_bias = pl.pallas_call(
        functools.partial(layout_kernel, norm_scale),
        out_shape=(
            shape((width, d_out), f32),
            shape((width, d_out), f32),
            shape((1, d_out), f32),
        ),
        in_specs=[in_vmem()] * 5,
        out_specs=(in_vmem(),) * 3,
        compiler_params=pltpu.CompilerParams(vmem_limit_bytes=8 * MIB),
        name="weight_layout",
    )(full, *near, far)

    grad_x = pl.pallas_call(
        end_kernel,
        out_shape=shape((v_local, width), bf16),
        in_specs=[in_vmem()] * 4,
        out_specs=in_vmem(),
        compiler_params=pltpu.CompilerParams(vmem_limit_bytes=8 * MIB),
        name="vertex_grads",
    )(index_row, back_arrived, grad_pre, weight_self)

    return output, grad_x, grad_self, grad_neigh, grad_bias.reshape(d_out)


def solution(mesh):
    in_specs = (
        P(AXES, None),
        P(AXES, None),
        P(),
        P(),
        P(),
        P(AXES, None, None),
        P(),
        P(AXES),
        P(AXES, None),
        P(AXES, None),
        P(AXES, None, None, None),
    )
    out_specs = (P(AXES, None), P(AXES, None), P(), P(), P())
    return jax.shard_map(
        per_device, mesh=mesh, in_specs=in_specs, out_specs=out_specs, check_vma=False
    )
```

```python
import functools
import math

import jax
import jax.numpy as jnp
from jax import lax
from jax.experimental import pallas as pl
from jax.experimental.pallas import tpu as pltpu
from jax.sharding import PartitionSpec as P

AXES = ("grp", "dom")
LANES = 128
EXACT = 256
MIB = 1 << 20
PIECES = 4
REST_ROOM = 24
GROUP = 8

NT = (((1,), (1,)), ((), ()))
TN = (((0,), (0,)), ((), ()))


def own_index():
    return lax.axis_index(AXES)


def own_group():
    return (lax.axis_index("dom") & 1) * 4 + (lax.axis_index("grp") & 3)


def dot32(a, b):
    return jnp.dot(a, b, preferred_element_type=jnp.float32)


def dot_general32(a, b, dims):
    return lax.dot_general(a, b, dims, preferred_element_type=jnp.float32)


def iota(shape, dim):
    return lax.broadcasted_iota(jnp.int32, shape, dim)


def rows_2d(block):
    peers, rows, width = block.shape
    if rows % 16 == 0:
        return block.reshape(peers * rows, width)
    return block.astype(jnp.float32).reshape(peers * rows, width).astype(block.dtype)


def rows_3d(block, rows):
    return block.reshape(block.shape[0] // rows, rows, block.shape[1]).astype(jnp.bfloat16)


class Pieces:
    def __init__(self, stage, target, sems, capacity):
        self.capacity = capacity
        self.stage, self.target, self.sems = stage, target, sems
        self.count = sems.shape[0]
        self.peers = stage.shape[0] // self.count
        self.copies = []

    def rows(self, piece):
        return slice(piece * self.peers, (piece + 1) * self.peers)

    def slots(self, piece):
        per_piece = self.peers * self.capacity
        return slice(piece * per_piece, (piece + 1) * per_piece)

    def start(self, piece):
        copy = pltpu.make_async_copy(
            self.stage.at[self.rows(piece)], self.target.at[self.rows(piece)], self.sems.at[piece]
        )
        copy.start()
        self.copies.append(copy)

    def send(self, piece, value):
        self.stage[self.rows(piece)] = value
        self.start(piece)

    def wait(self):
        for copy in self.copies:
            copy.wait()


def diagonal_row(spread, capacity):
    peers, slots = spread.shape
    own = iota((peers, slots), 1) // capacity == iota((peers, slots), 0)
    return jnp.sum(jnp.where(own, spread, 0.0), axis=0, keepdims=True)


def ones(mask):
    return mask.astype(jnp.float32).astype(jnp.bfloat16)


def one_hot(index_row, v_local):
    return ones(iota((v_local, index_row.shape[1]), 0) == index_row)


def as_column(index, slots):
    peers, capacity = index.shape
    spread = dot32(ones(iota((slots, peers), 0) // capacity == iota((slots, peers), 1)), index)
    own = iota((slots, capacity), 0) % capacity == iota((slots, capacity), 1)
    return jnp.sum(jnp.where(own, spread, 0.0), axis=1, keepdims=True).astype(jnp.int32)


def as_row(index, slots):
    capacity = index.shape[1]
    place = ones(iota((capacity, slots), 1) % capacity == iota((capacity, slots), 0))
    return diagonal_row(dot32(index, place), capacity).astype(jnp.int32)


def gather_kernel(
    rows_hbm,
    counts_hbm,
    features_hbm,
    dst_hbm,
    src_hbm,
    facts_ref,
    outgoing_ref,
    rows_ref,
    counts_ref,
    features_ref,
    dst_ref,
    src_ref,
    sems,
):
    moves = [
        pltpu.make_async_copy(source, target, sems.at[at])
        for at, (source, target) in enumerate(
            (
                (rows_hbm, rows_ref),
                (counts_hbm, counts_ref),
                (features_hbm, features_ref),
                (dst_hbm, dst_ref),
                (src_hbm, src_ref),
            )
        )
    ]
    for move in moves:
        move.start()
    moves[0].wait()
    moves[1].wait()
    peers, capacity = rows_ref.shape[1:]
    slots = peers * capacity
    v_local = features_ref.shape[0]
    counts = counts_ref[...]
    to_peer = jnp.sum(
        jnp.where(iota((peers, peers), 1) == own_index(), counts, 0), axis=1, keepdims=True
    )
    from_peer = jnp.sum(
        jnp.where(iota((peers, peers), 0) == own_index(), counts, 0), axis=0, keepdims=True
    )
    live = iota((peers, capacity), 1) < to_peer
    index = jnp.where(live, rows_ref[0], -1)
    column = as_column(index.astype(jnp.float32).astype(jnp.bfloat16), slots)
    hot = ones(iota((slots, v_local), 1) == column)
    moves[2].wait()
    outgoing_ref[...] = rows_3d(dot32(hot, features_ref[...]), capacity)

    for move in moves[3:]:
        move.wait()
    tiles = dst_ref.shape[1]
    facts_ref[0:1, :tiles] = dst_ref[...]
    facts_ref[1:2, :tiles] = src_ref[...]
    facts_ref[8 : 8 + peers, :capacity] = index
    facts_ref[8 + peers : 9 + peers, :peers] = from_peer


def build_kernel(
    buffers,
    chunk,
    peers,
    used_ref,
    facts_hbm,
    masks_ref,
    adj_ref,
    counted_ref,
    index_row_ref,
    rest_ref,
    total,
    held,
    stage,
    tiles_ref,
    facts_ref,
    sems,
    stage_sem,
    small_sems,
):
    moves = [
        pltpu.make_async_copy(source, target, small_sems.at[at])
        for at, (source, target) in enumerate(
            ((facts_hbm.at[:8], tiles_ref), (facts_hbm.at[8:], facts_ref))
        )
    ]
    for move in moves:
        move.start()
    tile = masks_ref.shape[1]
    slots = adj_ref.shape[0]
    blocks = slots // tile
    capacity = slots // peers

    def fetch(step):
        slot = lax.rem(step, buffers)
        return pltpu.make_async_copy(
            masks_ref.at[pl.ds(step * chunk, chunk)], held.at[slot], sems.at[slot]
        )

    for step in range(buffers):
        fetch(step).start()

    def clear(block, carry):
        total[block] = jnp.zeros((tile, tile), jnp.int32)
        return carry

    lax.fori_loop(0, blocks * blocks, clear, 0)
    for move in moves:
        move.wait()
    used = used_ref[0]
    chunks = (used + chunk - 1) // chunk

    def one_chunk(step, carry):
        slot = lax.rem(step, buffers)
        fetch(step).wait()
        first = step * chunk

        def one_tile(at, inner):
            where = tiles_ref[0, first + at] * blocks + tiles_ref[1, first + at]
            total[where] += held[slot, at]
            return inner

        full = first + chunk <= used

        @pl.when(full)
        def _():
            for at in range(chunk):
                one_tile(at, 0)

        @pl.when(jnp.logical_not(full))
        def _():
            lax.fori_loop(0, used - first, one_tile, 0)

        @pl.when(step + buffers < chunks)
        def _():
            fetch(step + buffers).start()

        return carry

    lax.fori_loop(0, chunks, one_chunk, 0)
    for step in range(buffers):

        @pl.when(step >= chunks)
        def _():
            fetch(step).wait()


    index = facts_ref[:peers, :capacity].astype(jnp.float32).astype(jnp.bfloat16)
    index_row_ref[...] = as_row(index, slots)
    live_count = facts_ref[peers : peers + 1, :peers].astype(jnp.float32)
    live_count = jnp.broadcast_to(live_count, (8, peers))
    place = iota((peers, slots), 1) // capacity == iota((peers, slots), 0)
    spread = dot32(
        live_count.astype(jnp.bfloat16), ones(place)
    )
    live_row = (iota((8, slots), 1) % capacity < spread.astype(jnp.int32)).astype(jnp.float32)

    def one_row(row, most):
        counted = jnp.zeros((tile, tile), jnp.float32)
        at_row = pl.multiple_of(row * tile, tile)
        for col in range(blocks):
            value = total[row * blocks + col]
            most = jnp.maximum(most, value)
            value = value.astype(jnp.float32)
            counted = counted + value * live_row[:1, col * tile : (col + 1) * tile]
            low = jnp.minimum(value, float(EXACT))
            adj_ref[pl.ds(at_row, tile), col * tile : (col + 1) * tile] = low.astype(jnp.bfloat16)
        counted_ref[pl.ds(row, 1), :] = jnp.sum(counted.T, axis=0, keepdims=True)
        return most

    most = lax.fori_loop(0, blocks, one_row, jnp.zeros((tile, tile), jnp.int32))
    over = jnp.max(most) > EXACT
    counted_ref[blocks:, :] = jnp.full((8, tile), over.astype(jnp.float32))

    @pl.when(over)
    def _():
        def rest_row(row, carry):
            for col in range(blocks):
                value = jnp.maximum(total[row * blocks + col] - EXACT, 0)
                stage[:, col * tile : (col + 1) * tile] = value.astype(jnp.float32).astype(
                    jnp.bfloat16
                )
            copy = pltpu.make_async_copy(
                stage, rest_ref.at[pl.ds(pl.multiple_of(row * tile, tile), tile)], stage_sem
            )
            copy.start()
            copy.wait()
            return carry

        lax.fori_loop(0, blocks, rest_row, 0)


def forward_kernel(
    adj_ref,
    counted_ref,
    mirrored_ref,
    rest_ref,
    out_hbm,
    out_ref,
    more,
    stage,
    stage_sem,
    sems,
):
    peers, capacity, width = mirrored_ref.shape
    slots = peers * capacity
    tile = stage.shape[0]
    columns = width // LANES
    source = rows_2d(mirrored_ref[...])
    counted = counted_ref[: slots // tile, :]
    over = jnp.max(counted_ref[slots // tile :, :]) > 0
    high = jnp.floor(counted * (1.0 / EXACT))
    low = counted - high * EXACT
    per_group = LANES // capacity
    at_extra = columns * capacity
    extra = out_ref.shape[1] - at_extra
    which = iota((extra, LANES), 0)
    for group in range(slots // LANES):
        both = jnp.where(
            which == 0,
            high[group : group + 1],
            jnp.where(which == 1, low[group : group + 1], 0.0),
        ).astype(jnp.bfloat16)
        out_ref[group * per_group : (group + 1) * per_group, at_extra:, :] = jnp.broadcast_to(
            both[None], (per_group, extra, LANES)
        )

    def multiply(add_rest):
        pieces = Pieces(out_ref, out_hbm, sems, capacity)
        for piece in range(pieces.count):
            sums = dot32(adj_ref[pieces.slots(piece), :], source)
            if add_rest:
                sums += more[pieces.slots(piece), :]
            for col in range(columns):
                out_ref[pieces.rows(piece), col * capacity : (col + 1) * capacity, :] = rows_3d(
                    sums[:, col * LANES : (col + 1) * LANES], capacity
                )
            pieces.start(piece)
        pieces.wait()

    @pl.when(jnp.logical_not(over))
    def _():
        multiply(False)

    @pl.when(over)
    def _():
        for row in range(slots // tile):
            rows = slice(row * tile, (row + 1) * tile)
            copy = pltpu.make_async_copy(rest_ref.at[rows], stage, stage_sem)
            copy.start()
            copy.wait()
            more[rows, :] = dot32(stage[...], source)
        multiply(True)


def middle_kernel(
    index_ref,
    arrived_ref,
    features_ref,
    cotangent_ref,
    weight_self_ref,
    weight_neigh_ref,
    bias_ref,
    output_ref,
    mean_ref,
    grad_pre_ref,
    out_ref,
):
    v_local, width = features_ref.shape
    peers = arrived_ref.shape[0]
    slots = index_ref.shape[1]
    capacity = slots // peers
    columns = width // LANES
    where = iota((v_local, slots), 0) == index_ref[...]
    hot = where.astype(jnp.float32).astype(jnp.bfloat16)

    extra = arrived_ref[:, columns * capacity :, :].astype(jnp.float32)
    both = jnp.concatenate([extra[:, 0, :], extra[:, 1, :]], axis=0).astype(jnp.bfloat16)
    section = lax.rem(own_index(), LANES // capacity) * capacity
    place = iota((LANES, slots), 0) == section + iota((LANES, slots), 1) % capacity
    spread = dot32(both, ones(place))
    counted = diagonal_row(spread[:peers] * float(EXACT) + spread[peers:], capacity)
    degrees = jnp.sum(jnp.where(where, counted, 0.0), axis=1, keepdims=True)
    divisor = jnp.maximum(degrees, 1.0)

    partial = jnp.concatenate(
        [
            rows_2d(arrived_ref[:, col * capacity : (col + 1) * capacity, :])
            for col in range(columns)
        ],
        axis=1,
    )
    mean_rows = (dot32(hot, partial) / divisor).astype(jnp.bfloat16)
    mean_ref[...] = mean_rows
    pre_act = (
        dot32(features_ref[...], weight_self_ref[...])
        + dot32(mean_rows, weight_neigh_ref[...])
        + bias_ref[...].astype(jnp.float32)
    )
    sigmoid_pre = 1.0 / (1.0 + jnp.exp(-pre_act))
    grad_pre32 = (
        cotangent_ref[...].astype(jnp.float32)
        * sigmoid_pre
        * (1.0 + pre_act * (1.0 - sigmoid_pre))
    )
    grad_pre = grad_pre32.astype(jnp.bfloat16)
    grad_mean = (dot_general32(grad_pre, weight_neigh_ref[...], NT) / divisor).astype(jnp.bfloat16)
    grad_pre_ref[...] = grad_pre
    output_ref[...] = (pre_act * sigmoid_pre).astype(jnp.bfloat16)
    out_ref[...] = rows_3d(dot_general32(hot, grad_mean, TN), capacity)


def parts_kernel(features_ref, mean_ref, grad_pre_ref, keep_ref, send_ref):
    grad_pre = grad_pre_ref[...]
    width, d_out = features_ref.shape[1], grad_pre.shape[1]
    rows = keep_ref.shape[0]
    block = 2 * rows // GROUP
    for kind, rows_ref in enumerate((features_ref, mean_ref)):
        part = dot_general32(rows_ref[...], grad_pre, TN)
        for col in range(d_out // LANES):
            for step in range(width // block):
                number = (col * 2 + kind) * (width // block) + step
                place = number ^ own_group()
                value = part[step * block : (step + 1) * block, col * LANES : (col + 1) * LANES]

                @pl.when(place < GROUP // 2)
                def _():
                    keep_ref[pl.ds(pl.multiple_of(place * block, block), block), :] = value

                @pl.when(place >= GROUP // 2)
                def _():
                    at = pl.multiple_of((place - GROUP // 2) * block, block)
                    send_ref[pl.ds(at, block), :] = value

    part_bias = jnp.sum(grad_pre.astype(jnp.float32), axis=0, keepdims=True)
    which = iota((8, LANES), 0)
    bias_block = jnp.zeros((8, LANES), jnp.float32)
    for col in range(d_out // LANES):
        bias_block = jnp.where(
            which == col, part_bias[:, col * LANES : (col + 1) * LANES], bias_block
        )
    send_ref[rows:, :] = bias_block


def quarter_kernel(keep_ref, sent_ref, got_ref, own_ref, *other_refs):
    rows = keep_ref.shape[0]
    block = rows // 4
    bias = (sent_ref[rows:, :] + got_ref[rows:, :]).astype(jnp.bfloat16)
    for at, ref in enumerate((own_ref, *other_refs)):
        cut = slice(at * block, (at + 1) * block)
        ref[:block, :] = (keep_ref[cut, :] + got_ref[cut, :]).astype(ref.dtype)
        ref[block:, :] = bias.astype(ref.dtype)


def backward_kernel(
    adj_ref, counted_ref, arrived_ref, rest_ref, out_hbm, out_ref, more, stage, stage_sem, sems
):
    peers, capacity, width = arrived_ref.shape
    tile = stage.shape[0]
    slots = peers * capacity
    source = rows_2d(arrived_ref[...])
    over = jnp.max(counted_ref[slots // tile :, :]) > 0
    source_t = source.astype(jnp.float32).T.astype(jnp.bfloat16)

    def multiply(add_rest):
        pieces = Pieces(out_ref, out_hbm, sems, capacity)
        for piece in range(pieces.count):
            sums = dot32(source_t, adj_ref[:, pieces.slots(piece)]).T
            if add_rest:
                sums += more[pieces.slots(piece), :]
            pieces.send(piece, rows_3d(sums, capacity))
        pieces.wait()

    @pl.when(jnp.logical_not(over))
    def _():
        multiply(False)

    @pl.when(over)
    def _():
        more[...] = jnp.zeros_like(more)
        for row in range(slots // tile):
            rows = slice(row * tile, (row + 1) * tile)
            copy = pltpu.make_async_copy(rest_ref.at[rows], stage, stage_sem)
            copy.start()
            copy.wait()
            more[...] += dot_general32(stage[...], source[rows], TN)
        multiply(True)


def layout_kernel(
    norm_scale,
    own_ref,
    near_1_ref,
    near_2_ref,
    near_3_ref,
    far_ref,
    self_ref,
    neigh_ref,
    bias_ref,
):
    block = near_1_ref.shape[0]
    near_refs = (near_1_ref, near_2_ref, near_3_ref)
    width, d_out = self_ref.shape
    per_part = width // block
    for place in range(GROUP):
        if place < 1:
            value = own_ref[:block, :]
        elif place < 4:
            value = near_refs[place - 1][...]
        else:
            value = far_ref[(place - 4) * block : (place - 3) * block, :]
        value = value.astype(jnp.float32) * norm_scale
        number = place ^ own_group()
        at = pl.multiple_of(lax.rem(number, per_part) * block, block)
        quarter = number // per_part
        for col in range(d_out // LANES):
            for kind, ref in enumerate((self_ref, neigh_ref)):

                @pl.when(quarter == col * 2 + kind)
                def _():
                    ref[pl.ds(at, block), col * LANES : (col + 1) * LANES] = value

    for col in range(d_out // LANES):
        bias_ref[:, col * LANES : (col + 1) * LANES] = (
            own_ref[block + col : block + col + 1, :].astype(jnp.float32) * norm_scale
        )


def end_kernel(index_ref, arrived_ref, grad_pre_ref, weight_self_ref, grad_x_ref):
    v_local = grad_x_ref.shape[0]
    hot = one_hot(index_ref[...], v_local)
    own = dot_general32(grad_pre_ref[...], weight_self_ref[...], NT)
    back = dot32(hot, rows_2d(arrived_ref[...]))
    grad_x_ref[...] = (own + back).astype(jnp.bfloat16)


def in_smem():
    return pl.BlockSpec(memory_space=pltpu.SMEM)


def in_vmem():
    return pl.BlockSpec(memory_space=pltpu.VMEM)


def in_hbm():
    return pl.BlockSpec(memory_space=pltpu.HBM)


def exchange(block):
    return lax.all_to_all(block, AXES, split_axis=0, concat_axis=0, tiled=True)


def swap(block, axis, bit):
    size = lax.axis_size(axis)
    return lax.ppermute(block, axis, [(at, at ^ bit) for at in range(size)])


def per_device(
    features,
    cotangent,
    weight_self,
    weight_neigh,
    layer_bias,
    mirror_rows,
    mirror_counts,
    tile_count,
    tile_rows,
    tile_cols,
    tile_masks,
):
    f32, bf16, i32 = jnp.float32, jnp.bfloat16, jnp.int32
    v_local, width = features.shape
    d_out = weight_self.shape[1]
    peers, capacity = mirror_rows.shape[1:]
    slots = peers * capacity
    masks = tile_masks[0]
    tiles_max, tile = masks.shape[:2]
    blocks = slots // tile
    pieces = width // LANES
    rows = 2 * width * (d_out // LANES)
    shape = jax.ShapeDtypeStruct

    facts_shape = (8 + peers + 8, -(-tiles_max // LANES) * LANES)
    facts, outgoing = pl.pallas_call(
        gather_kernel,
        out_shape=(shape(facts_shape, i32), shape((peers, capacity, width), bf16)),
        in_specs=[in_hbm()] * 5,
        out_specs=(in_vmem(), in_vmem()),
        scratch_shapes=[
            pltpu.VMEM(mirror_rows.shape, i32),
            pltpu.VMEM(mirror_counts.shape, i32),
            pltpu.VMEM(features.shape, bf16),
            pltpu.VMEM(tile_rows.shape, i32),
            pltpu.VMEM(tile_cols.shape, i32),
            pltpu.SemaphoreType.DMA((5,)),
        ],
        compiler_params=pltpu.CompilerParams(vmem_limit_bytes=60 * MIB),
        name="gather_rows",
    )(mirror_rows, mirror_counts, features, tile_rows, tile_cols)

    mirrored = exchange(outgoing)

    chunk = math.gcd(8, tiles_max)
    buffers = min(8, tiles_max // chunk)
    adj, counted, index_row, rest = pl.pallas_call(
        functools.partial(build_kernel, buffers, chunk, peers),
        out_shape=(
            shape((slots, slots), bf16),
            shape((blocks + 8, tile), f32),
            shape((1, slots), i32),
            shape((REST_ROOM * slots, slots), bf16),
        ),
        in_specs=[in_smem()] + [in_hbm()] * 2,
        out_specs=(in_vmem(),) * 3 + (in_hbm(),),
        scratch_shapes=[
            pltpu.VMEM((blocks * blocks, tile, tile), i32),
            pltpu.VMEM((buffers, chunk, tile, tile), i32),
            pltpu.VMEM((tile, slots), bf16),
            pltpu.SMEM((8, facts_shape[1]), i32),
            pltpu.VMEM((facts_shape[0] - 8, facts_shape[1]), i32),
            pltpu.SemaphoreType.DMA((buffers,)),
            pltpu.SemaphoreType.DMA,
            pltpu.SemaphoreType.DMA((2,)),
        ],
        compiler_params=pltpu.CompilerParams(vmem_limit_bytes=48 * MIB),
        cost_estimate=pl.CostEstimate(
            flops=4 * tiles_max * tile * tile,
            bytes_accessed=masks.size * 4,
            transcendentals=0,
        ),
        name="build_counts",
    )(tile_count, facts, masks)

    partial_shape = (peers, pieces * capacity + 8, LANES)
    partial = pl.pallas_call(
        forward_kernel,
        out_shape=shape(partial_shape, bf16),
        in_specs=[in_vmem(), in_vmem(), in_vmem(), in_hbm()],
        out_specs=in_hbm(),
        scratch_shapes=[
            pltpu.VMEM(partial_shape, bf16),
            pltpu.VMEM((slots, width), f32),
            pltpu.VMEM((tile, slots), bf16),
            pltpu.SemaphoreType.DMA,
            pltpu.SemaphoreType.DMA((PIECES,)),
        ],
        compiler_params=pltpu.CompilerParams(vmem_limit_bytes=40 * MIB),
        name="forward_sums",
    )(adj, counted, mirrored, rest)

    arrived = exchange(partial)

    output, mean_rows, grad_pre, sent_back = pl.pallas_call(
        middle_kernel,
        out_shape=(
            shape((v_local, d_out), bf16),
            shape((v_local, width), bf16),
            shape((v_local, d_out), bf16),
            shape((peers, capacity, width), bf16),
        ),
        in_specs=[in_vmem()] * 7,
        out_specs=(in_vmem(),) * 4,
        compiler_params=pltpu.CompilerParams(vmem_limit_bytes=12 * MIB),
        name="vertex_update",
    )(
        index_row,
        arrived,
        features,
        cotangent,
        weight_self,
        weight_neigh,
        layer_bias.reshape(1, d_out),
    )

    mirrored_grads = exchange(sent_back)

    keep, send = pl.pallas_call(
        parts_kernel,
        out_shape=(
            shape((rows // 2, LANES), f32),
            shape((rows // 2 + 8, LANES), f32),
        ),
        in_specs=[in_vmem()] * 3,
        out_specs=(in_vmem(),) * 2,
        compiler_params=pltpu.CompilerParams(vmem_limit_bytes=8 * MIB),
        cost_estimate=pl.CostEstimate(flops=1 << 27, bytes_accessed=1 << 20, transcendentals=0),
        name="weight_parts",
    )(features, mean_rows, grad_pre)

    got = swap(send, "dom", 1)
    own, *others = pl.pallas_call(
        quarter_kernel,
        out_shape=tuple(shape((rows // GROUP + 8, LANES), kind) for kind in (f32, bf16, bf16, bf16)),
        in_specs=[in_vmem()] * 3,
        out_specs=(in_vmem(),) * 4,
        compiler_params=pltpu.CompilerParams(vmem_limit_bytes=4 * MIB),
        name="quarter_sums",
    )(keep, send, got)
    got = [swap(other, "grp", bit) for bit, other in zip((1, 2, 3), others, strict=True)]
    full = (own + got[0].astype(f32)) + (got[1].astype(f32) + got[2].astype(f32))
    bit = 2
    while bit < lax.axis_size("dom"):
        sent = full.astype(bf16)
        got = [
            swap(sent, "dom", other)
            for other in (bit, 2 * bit, 3 * bit)
            if other < lax.axis_size("dom")
        ]
        wide = [value.astype(f32) for value in (sent, *got)]
        full = wide[0] + wide[1]
        if len(wide) == 4:
            full = full + (wide[2] + wide[3])
        bit *= 4
    full, mirrored_grads = lax.optimization_barrier((full, mirrored_grads))
    back_partial = pl.pallas_call(
        backward_kernel,
        out_shape=shape((peers, capacity, width), bf16),
        in_specs=[in_vmem(), in_vmem(), in_vmem(), in_hbm()],
        out_specs=in_hbm(),
        scratch_shapes=[
            pltpu.VMEM((peers, capacity, width), bf16),
            pltpu.VMEM((slots, width), f32),
            pltpu.VMEM((tile, slots), bf16),
            pltpu.SemaphoreType.DMA,
            pltpu.SemaphoreType.DMA((PIECES,)),
        ],
        compiler_params=pltpu.CompilerParams(vmem_limit_bytes=8 * MIB),
        cost_estimate=pl.CostEstimate(flops=1 << 29, bytes_accessed=3 << 20, transcendentals=0),
        name="backward_sums",
    )(adj, counted, mirrored_grads, rest)

    back_arrived = exchange(back_partial)

    full = full.astype(bf16)
    block = full[: rows // GROUP]
    near = [swap(block, "grp", bit) for bit in (1, 2, 3)]
    far = swap(jnp.concatenate([block, *near]), "dom", 1)

    norm_scale = 1.0 / math.sqrt(v_local * peers)
    grad_self, grad_neigh, grad_bias = pl.pallas_call(
        functools.partial(layout_kernel, norm_scale),
        out_shape=(
            shape((width, d_out), f32),
            shape((width, d_out), f32),
            shape((1, d_out), f32),
        ),
        in_specs=[in_vmem()] * 5,
        out_specs=(in_vmem(),) * 3,
        compiler_params=pltpu.CompilerParams(vmem_limit_bytes=8 * MIB),
        name="weight_layout",
    )(full, *near, far)

    grad_x = pl.pallas_call(
        end_kernel,
        out_shape=shape((v_local, width), bf16),
        in_specs=[in_vmem()] * 4,
        out_specs=in_vmem(),
        compiler_params=pltpu.CompilerParams(vmem_limit_bytes=8 * MIB),
        name="vertex_grads",
    )(index_row, back_arrived, grad_pre, weight_self)

    return output, grad_x, grad_self, grad_neigh, grad_bias.reshape(d_out)


def solution(mesh):
    in_specs = (
        P(AXES, None),
        P(AXES, None),
        P(),
        P(),
        P(),
        P(AXES, None, None),
        P(),
        P(AXES),
        P(AXES, None),
        P(AXES, None),
        P(AXES, None, None, None),
    )
    out_specs = (P(AXES, None), P(AXES, None), P(), P(), P())
    return jax.shard_map(
        per_device, mesh=mesh, in_specs=in_specs, out_specs=out_specs, check_vma=False
    )
```
